256 devices in a mesh: dp: 8 (over y, core), seq: 32 (over x, z).
Axes of the slice: x: 4, y: 4, z: 8, core: 2. Of those that a mesh axis runs over, the one named last changes fastest.
Arguments:
- queries: bfloat16 [8, 4096, 1536], P('dp', 'seq'), may hold values from -6 to 6
- key_rows: bfloat16 [8, 4096, 512], P('dp', 'seq'), may hold values from -6 to 6
- value_rows: bfloat16 [8, 4096, 512], P('dp', 'seq'), may hold values from -6 to 6
- out_grad: bfloat16 [8, 4096, 1536], P('dp', 'seq'), may hold values from -6 to 6
- query_map: bfloat16 [12, 128, 64], replicated, may hold values from -40 to 40
- key_map: bfloat16 [12, 128, 64], replicated, may hold values from -40 to 40
Outputs:
- attended: bfloat16 [8, 4096, 1536], P('dp', 'seq')
- query_grad: bfloat16 [8, 4096, 1536], P('dp', 'seq')
- key_grad: bfloat16 [8, 4096, 512], P('dp', 'seq')
- value_grad: bfloat16 [8, 4096, 512], P('dp', 'seq')
- query_map_grad: float32 [12, 128, 64], replicated
- key_map_grad: float32 [12, 128, 64], replicated
The draws below stay inside these ranges and needn't reach their ends.
All inputs are finite; a program needn't handle non-finite values.
Results may differ from the reference program's by a relative error of at most 0.013.
Values sent between devices are 32-bit elements; how exact they have to be, the bound alone decides.
No kernel may reach another device: no remote copies, remote signals or barrier semaphores. Data moves between devices by JAX's collectives and lax.ppermute only.
A program may use at most 128 MiB of HBM per device.

```python
import math
import jax
import jax.numpy as jnp
from jax import lax

H = 12
KVH = 4
DH = 128
FH = 64
TOK_DEV = 128
BATCH = 8
SEQLEN = 4096
N_SEQ = 32


def draw_query_map(key, part):
    key = jax.random.fold_in(key, 11)
    base_key = jax.random.fold_in(key, 0)
    weights = jnp.clip(jax.random.normal(base_key, (H, DH, FH), jnp.float32), -4.0, 4.0) * (1.5 / math.sqrt(DH))
    return weights.astype(jnp.bfloat16)


def draw_key_map(key, part):
    key = jax.random.fold_in(key, 23)
    base_key = jax.random.fold_in(key, 0)
    weights = jnp.clip(jax.random.normal(base_key, (H, DH, FH), jnp.float32), -4.0, 4.0) * (1.5 / math.sqrt(DH))
    return weights.astype(jnp.bfloat16)


def block_levels(key, dims, shards, low, high):
    def one(dim, shards_of):
        draws = jax.random.uniform(jax.random.fold_in(jax.random.fold_in(key, 6), dim), (shards_of,), jnp.float32, low / len(shards), high / len(shards))
        return jnp.repeat(jnp.exp(draws), dims[dim] // shards_of).reshape((-1,) + (1,) * (len(dims) - dim - 1))

    factor_of = one(*shards[0])
    for cut in shards[1:]:
        factor_of = factor_of * one(*cut)
    return factor_of


def normal_values(stream_key, extent, scale, limit, cuts=(), held_as=jnp.bfloat16):
    array = scale * jax.random.normal(stream_key, extent, jnp.float32)
    if cuts:
        array = array * block_levels(stream_key, extent, cuts, -0.22, 0.18)
    return jnp.clip(array, -limit, limit).astype(held_as)


def setup_inputs(seed: int = 0) -> dict:
    streams_of = jax.random.split(jax.random.key(seed), 7)
    queries = normal_values(streams_of[0], (BATCH, SEQLEN, H * DH), 1.0, 6.0, ((0, 8), (1, 32)))
    key_rows = normal_values(streams_of[1], (BATCH, SEQLEN, KVH * DH), 1.0, 6.0, ((0, 8), (1, 32)))
    value_rows = normal_values(streams_of[2], (BATCH, SEQLEN, KVH * DH), 1.0, 6.0, ((0, 8), (1, 32)))
    out_grad = normal_values(streams_of[3], (BATCH, SEQLEN, H * DH), 1.0, 6.0, ((0, 8), (1, 32)))
    query_map = draw_query_map(jax.random.fold_in(streams_of[6], 71), 0)
    key_map = draw_key_map(jax.random.fold_in(streams_of[6], 71), 0)
    return {"queries": queries, "key_rows": key_rows, "value_rows": value_rows, "out_grad": out_grad, "query_map": query_map, "key_map": key_map}


def mix(form, left, right):
    return jnp.einsum(form, left.astype(jnp.float32), right.astype(jnp.float32), precision=lax.Precision.HIGHEST)


def fine(form, left, right):
    return jnp.einsum(form, left, right, precision=lax.Precision.HIGHEST)


def feature_map(inputs, weight):
    doubled = jnp.concatenate([weight, -weight], axis=-1)
    scores = mix('thd,hdf->htf', inputs, doubled)
    heads, tokens, width = scores.shape
    halves = scores.reshape(heads, tokens, 2, width // 2)
    return jax.nn.softmax(halves, axis=-1).reshape(heads, tokens, width)


def prepare(query_block, key_block, value_block, query_map, key_map):
    tokens = query_block.shape[0]
    group_size = H // KVH
    query_heads = query_block.reshape(tokens, H, DH)
    key_heads = jnp.repeat(key_block.reshape(tokens, KVH, DH), group_size, axis=1)
    value_heads = jnp.repeat(value_block.reshape(tokens, KVH, DH), group_size, axis=1)
    prob_query = feature_map(query_heads, query_map)
    prob_key = feature_map(key_heads, key_map)
    feat_query = prob_query.astype(jnp.bfloat16)
    feat_key = prob_key.astype(jnp.bfloat16)
    local_state = mix('hsf,shd->hfd', feat_key, value_heads)
    local_norm = jnp.sum(feat_key.astype(jnp.float32), axis=1)
    return dict(query_heads=query_heads, key_heads=key_heads, value_heads=value_heads, prob_query=prob_query, prob_key=prob_key, feat_query=feat_query, feat_key=feat_key, local_state=local_state, local_norm=local_norm)


def finish(prepared, grad_block, prefix_state, prefix_norm):
    feat_query = prepared["feat_query"]
    feat_key = prepared["feat_key"]
    value_heads = prepared["value_heads"]
    tokens = feat_query.shape[1]
    causal = jnp.arange(tokens)[:, None] >= jnp.arange(tokens)[None, :]
    scores = jnp.where(causal[None], mix('htf,hsf->hts', feat_query, feat_key), 0.0)
    scores_low = scores.astype(jnp.bfloat16)
    state_low = prefix_state.astype(jnp.bfloat16)
    denominator = jnp.sum(scores, axis=-1) + fine('htf,hf->ht', feat_query.astype(jnp.float32), prefix_norm)
    numerator = mix('hts,shd->thd', scores_low, value_heads) + mix('htf,hfd->thd', feat_query, state_low)
    row_scale = denominator.T[:, :, None]
    out_full = numerator / row_scale
    grad_full = grad_block.reshape(tokens, H, DH).astype(jnp.float32)
    grad_num = (grad_full / row_scale).astype(jnp.bfloat16)
    grad_den = -jnp.sum(grad_full * out_full, axis=-1) / denominator.T
    carry_state = mix('htf,thd->hfd', feat_query, grad_num)
    carry_norm = fine('htf,th->hf', feat_query.astype(jnp.float32), grad_den)
    attended = out_full.reshape(tokens, H * DH).astype(jnp.bfloat16)
    return dict(attended=attended, scores_low=scores_low, state_low=state_low, grad_num=grad_num, grad_den=grad_den, carry_state=carry_state, carry_norm=carry_norm)


def map_back(softened, grad_feat, inputs, weight):
    heads, tokens, width = softened.shape
    halves = softened.reshape(heads, tokens, 2, width // 2)
    grad_halves = grad_feat.reshape(heads, tokens, 2, width // 2)
    inner = jnp.sum(halves * grad_halves, axis=-1, keepdims=True)
    grad_scores = halves * (grad_halves - inner)
    grad_low = (grad_scores[:, :, 0] - grad_scores[:, :, 1]).astype(jnp.bfloat16)
    weight_grad = mix('thd,htf->hdf', inputs, grad_low)
    input_grad = mix('htf,hdf->thd', grad_low, weight)
    return weight_grad, input_grad


def gradients(prepared, finished, prefix_norm, back_state, back_norm, query_map, key_map):
    feat_query = prepared["feat_query"]
    feat_key = prepared["feat_key"]
    value_heads = prepared["value_heads"]
    grad_num = finished["grad_num"]
    tokens = feat_query.shape[1]
    group_size = H // KVH
    causal = jnp.arange(tokens)[:, None] >= jnp.arange(tokens)[None, :]
    den_rows = finished["grad_den"].T
    dscore = jnp.where(causal[None], mix('thd,shd->hts', grad_num, value_heads) + den_rows[:, :, None], 0.0)
    dscore_low = dscore.astype(jnp.bfloat16)
    back_low = back_state.astype(jnp.bfloat16)
    grad_feat_query = mix('hts,hsf->htf', dscore_low, feat_key) + mix('thd,hfd->htf', grad_num, finished["state_low"]) + den_rows[:, :, None] * prefix_norm[:, None, :]
    grad_feat_key = mix('hts,htf->hsf', dscore_low, feat_query) + mix('shd,hfd->hsf', value_heads, back_low) + back_norm[:, None, :]
    grad_value = mix('hts,thd->shd', finished["scores_low"], grad_num) + mix('hsf,hfd->shd', feat_key, back_low)
    value_grad = grad_value.reshape(tokens, KVH, group_size, DH).sum(2).reshape(tokens, KVH * DH).astype(jnp.bfloat16)
    query_weight_grad, query_input = map_back(prepared["prob_query"], grad_feat_query, prepared["query_heads"], query_map)
    key_weight_grad, key_input = map_back(prepared["prob_key"], grad_feat_key, prepared["key_heads"], key_map)
    query_grad = query_input.reshape(tokens, H * DH).astype(jnp.bfloat16)
    key_grad = key_input.reshape(tokens, KVH, group_size, DH).sum(2).reshape(tokens, KVH * DH).astype(jnp.bfloat16)
    return query_grad, key_grad, value_grad, query_weight_grad, key_weight_grad


def suffix_sum(stacked):
    inclusive = jnp.flip(jnp.cumsum(jnp.flip(stacked, 0), 0), 0)
    return jnp.concatenate([inclusive[1:], jnp.zeros_like(inclusive[:1])], 0)


def reference(queries, key_rows, value_rows, out_grad, query_map, key_map):
    def one_sequence(pieces):
        query_seq, key_seq, value_seq, grad_seq = pieces
        blocks = (query_seq.reshape(N_SEQ, TOK_DEV, H * DH), key_seq.reshape(N_SEQ, TOK_DEV, KVH * DH), value_seq.reshape(N_SEQ, TOK_DEV, KVH * DH), grad_seq.reshape(N_SEQ, TOK_DEV, H * DH))
        initial = (jnp.zeros((H, 2 * FH, DH), jnp.float32), jnp.zeros((H, 2 * FH), jnp.float32))

        def forward_step(running, block_rows):
            prefix_state, prefix_norm = running
            prepared = prepare(block_rows[0], block_rows[1], block_rows[2], query_map, key_map)
            finished = finish(prepared, block_rows[3], prefix_state, prefix_norm)
            following = (prefix_state + prepared["local_state"], prefix_norm + prepared["local_norm"])
            return following, (finished["attended"], prefix_state, prefix_norm, finished["carry_state"], finished["carry_norm"])

        _, (outputs, states, norms, carries, carry_norms) = lax.scan(forward_step, initial, blocks)
        back_states = suffix_sum(carries)
        back_norms = suffix_sum(carry_norms)

        def backward_step(block_rows):
            prepared = prepare(block_rows[0], block_rows[1], block_rows[2], query_map, key_map)
            finished = finish(prepared, block_rows[3], block_rows[4], block_rows[5])
            return gradients(prepared, finished, block_rows[5], block_rows[6], block_rows[7], query_map, key_map)

        query_grad, key_grad, value_grad, query_weight, key_weight = lax.map(backward_step, blocks + (states, norms, back_states, back_norms))
        return (outputs.reshape(SEQLEN, H * DH), query_grad.reshape(SEQLEN, H * DH), key_grad.reshape(SEQLEN, KVH * DH), value_grad.reshape(SEQLEN, KVH * DH), jnp.sum(query_weight, axis=0), jnp.sum(key_weight, axis=0))

    results = lax.map(one_sequence, (queries, key_rows, value_rows, out_grad))
    return (results[0], results[1], results[2], results[3], jnp.sum(results[4], axis=0), jnp.sum(results[5], axis=0))
```

```python
import jax
import jax.numpy as jnp
from jax import lax
from jax.sharding import Mesh, PartitionSpec as P

H = 12
KVH = 4
DH = 128


def mix(form, left, right):
    return jnp.einsum(form, left, right, preferred_element_type=jnp.float32)


def fine(form, left, right):
    return jnp.einsum(form, left, right, precision=lax.Precision.HIGHEST)


def feature_map(inputs, weight):
    doubled = jnp.concatenate([weight, -weight], axis=-1)
    scores = mix("thd,hdf->htf", inputs, doubled)
    heads, tokens, width = scores.shape
    halves = scores.reshape(heads, tokens, 2, width // 2)
    return jax.nn.softmax(halves, axis=-1).reshape(heads, tokens, width)


def prepare(query_block, key_block, value_block, query_map, key_map):
    tokens = query_block.shape[0]
    group_size = H // KVH
    query_heads = query_block.reshape(tokens, H, DH)
    key_heads = jnp.repeat(key_block.reshape(tokens, KVH, DH), group_size, axis=1)
    value_heads = jnp.repeat(value_block.reshape(tokens, KVH, DH), group_size, axis=1)
    prob_query = feature_map(query_heads, query_map)
    prob_key = feature_map(key_heads, key_map)
    feat_query = prob_query.astype(jnp.bfloat16)
    feat_key = prob_key.astype(jnp.bfloat16)
    local_state = mix("hsf,shd->hfd", feat_key, value_heads)
    local_norm = jnp.sum(feat_key.astype(jnp.float32), axis=1)
    return dict(
        query_heads=query_heads,
        key_heads=key_heads,
        value_heads=value_heads,
        prob_query=prob_query,
        prob_key=prob_key,
        feat_query=feat_query,
        feat_key=feat_key,
        local_state=local_state,
        local_norm=local_norm,
    )


def weigh(prepared, grad_block, prefix_norm):
    feat_query = prepared["feat_query"]
    feat_key = prepared["feat_key"]
    tokens = feat_query.shape[1]
    causal = jnp.arange(tokens)[:, None] >= jnp.arange(tokens)[None, :]
    scores = jnp.where(causal[None], mix("htf,hsf->hts", feat_query, feat_key), 0.0)
    scores_low = scores.astype(jnp.bfloat16)
    denominator = jnp.sum(scores, axis=-1) + fine(
        "htf,hf->ht", feat_query.astype(jnp.float32), prefix_norm
    )
    row_scale = denominator.T[:, :, None]
    grad_full = grad_block.reshape(tokens, H, DH).astype(jnp.float32)
    grad_num = (grad_full / row_scale).astype(jnp.bfloat16)
    carry_state = mix("htf,thd->hfd", feat_query, grad_num)
    return dict(
        scores_low=scores_low,
        denominator=denominator,
        row_scale=row_scale,
        grad_full=grad_full,
        grad_num=grad_num,
        carry_state=carry_state,
    )


def finish(prepared, weighed, prefix_state):
    feat_query = prepared["feat_query"]
    tokens = feat_query.shape[1]
    state_low = prefix_state.astype(jnp.bfloat16)
    numerator = mix("hts,shd->thd", weighed["scores_low"], prepared["value_heads"]) + mix(
        "htf,hfd->thd", feat_query, state_low
    )
    out_full = numerator / weighed["row_scale"]
    grad_den = -jnp.sum(weighed["grad_full"] * out_full, axis=-1) / weighed["denominator"].T
    carry_norm = fine("htf,th->hf", feat_query.astype(jnp.float32), grad_den)
    attended = out_full.reshape(tokens, H * DH).astype(jnp.bfloat16)
    return dict(
        attended=attended,
        scores_low=weighed["scores_low"],
        state_low=state_low,
        grad_num=weighed["grad_num"],
        grad_den=grad_den,
        carry_norm=carry_norm,
    )


def map_back(softened, grad_feat, inputs, weight):
    heads, tokens, width = softened.shape
    halves = softened.reshape(heads, tokens, 2, width // 2)
    grad_halves = grad_feat.reshape(heads, tokens, 2, width // 2)
    inner = jnp.sum(halves * grad_halves, axis=-1, keepdims=True)
    grad_scores = halves * (grad_halves - inner)
    grad_low = (grad_scores[:, :, 0] - grad_scores[:, :, 1]).astype(jnp.bfloat16)
    weight_grad = mix("thd,htf->hdf", inputs, grad_low)
    input_grad = mix("htf,hdf->thd", grad_low, weight)
    return (weight_grad, input_grad)


def gradients(prepared, finished, prefix_norm, back_state, back_norm, query_map, key_map):
    feat_query = prepared["feat_query"]
    feat_key = prepared["feat_key"]
    value_heads = prepared["value_heads"]
    grad_num = finished["grad_num"]
    tokens = feat_query.shape[1]
    group_size = H // KVH
    causal = jnp.arange(tokens)[:, None] >= jnp.arange(tokens)[None, :]
    den_rows = finished["grad_den"].T
    dscore = jnp.where(
        causal[None], mix("thd,shd->hts", grad_num, value_heads) + den_rows[:, :, None], 0.0
    )
    dscore_low = dscore.astype(jnp.bfloat16)
    back_low = back_state.astype(jnp.bfloat16)
    grad_feat_query = (
        mix("hts,hsf->htf", dscore_low, feat_key)
        + mix("thd,hfd->htf", grad_num, finished["state_low"])
        + den_rows[:, :, None] * prefix_norm[:, None, :]
    )
    grad_feat_key = (
        mix("hts,htf->hsf", dscore_low, feat_query)
        + mix("shd,hfd->hsf", value_heads, back_low)
        + back_norm[:, None, :]
    )
    grad_value = mix("hts,thd->shd", finished["scores_low"], grad_num) + mix(
        "hsf,hfd->shd", feat_key, back_low
    )
    value_grad = (
        grad_value.reshape(tokens, KVH, group_size, DH)
        .sum(2)
        .reshape(tokens, KVH * DH)
        .astype(jnp.bfloat16)
    )
    query_weight_grad, query_input = map_back(
        prepared["prob_query"], grad_feat_query, prepared["query_heads"], query_map
    )
    key_weight_grad, key_input = map_back(
        prepared["prob_key"], grad_feat_key, prepared["key_heads"], key_map
    )
    query_grad = query_input.reshape(tokens, H * DH).astype(jnp.bfloat16)
    key_grad = (
        key_input.reshape(tokens, KVH, group_size, DH)
        .sum(2)
        .reshape(tokens, KVH * DH)
        .astype(jnp.bfloat16)
    )
    return (query_grad, key_grad, value_grad, query_weight_grad, key_weight_grad)


N_SEQ = 32
ROWS = H * DH // N_SEQ
SEQ = ("x", "z")


def exchange(blocks, axes=SEQ):
    return lax.all_to_all(blocks, axes, 0, 0, tiled=True)


def to_all(rows):
    padded = jnp.pad(rows, ((0, 16 - H), (0, 0)))
    return jnp.broadcast_to(padded[None], (N_SEQ,) + padded.shape)


def sum_before(parts):
    inclusive = jnp.cumsum(parts, axis=0)
    return jnp.concatenate([jnp.zeros_like(parts[:1]), inclusive[:-1]], 0)


def sum_after(parts):
    return sum_before(parts[::-1])[::-1]


def summed_everywhere(values):
    core = lax.axis_index("core")
    halves = values.reshape(2, -1, DH)
    mine = lax.dynamic_index_in_dim(halves, core, 0, False)
    other = lax.dynamic_index_in_dim(halves, 1 - core, 0, False)
    swap = [(0, 1), (1, 0)]
    mine = mine + lax.ppermute(other, "core", swap)
    part = exchange(mine.reshape(N_SEQ, -1, DH)).sum(0)
    total = part
    for step in range(1, 4):
        total = total + lax.ppermute(part, "y", [(i, (i + step) % 4) for i in range(4)])
    half = exchange(jnp.broadcast_to(total[None], (N_SEQ,) + total.shape)).reshape(-1, DH)
    swapped = lax.ppermute(half, "core", swap)
    low = jnp.where(core == 0, half, swapped)
    high = jnp.where(core == 0, swapped, half)
    return jnp.concatenate([low, high], 0)


def shards(queries, key_rows, value_rows, out_grad, query_map, key_map):
    me = lax.axis_index(SEQ)
    order = jnp.arange(N_SEQ)[:, None, None]
    prepared = prepare(queries[0], key_rows[0], value_rows[0], query_map, key_map)
    local_state = prepared["local_state"].reshape(N_SEQ, ROWS, DH)
    first = exchange(jnp.concatenate([local_state, to_all(prepared["local_norm"])], 1))
    prefix_norm = jnp.sum(jnp.where(order < me, first[:, ROWS : ROWS + H], 0.0), 0)
    weighed = weigh(prepared, out_grad[0], prefix_norm)
    carry_state = weighed["carry_state"].reshape(N_SEQ, ROWS, DH)
    second = exchange(jnp.concatenate([sum_before(first[:, :ROWS]), carry_state], 1))
    prefix_state = second[:, :ROWS].reshape(H, DH, DH)
    finished = finish(prepared, weighed, prefix_state)
    third = exchange(
        jnp.concatenate([sum_after(second[:, ROWS:]), to_all(finished["carry_norm"])], 1)
    )
    back_state = third[:, :ROWS].reshape(H, DH, DH)
    back_norm = jnp.sum(jnp.where(order > me, third[:, ROWS : ROWS + H], 0.0), 0)
    query_grad, key_grad, value_grad, query_weight_grad, key_weight_grad = gradients(
        prepared, finished, prefix_norm, back_state, back_norm, query_map, key_map
    )
    weights = jnp.stack([query_weight_grad, key_weight_grad])
    totals = summed_everywhere(weights.reshape(-1, DH)).reshape(weights.shape)
    return (
        finished["attended"][None],
        query_grad[None],
        key_grad[None],
        value_grad[None],
        totals[0],
        totals[1],
    )


ROWS_SPLIT = P(("y", "core"), ("x", "z"), None)


def solution(mesh):
    fine_mesh = Mesh(mesh.devices.reshape(4, 2, 4, 8), ("y", "core", "x", "z"))
    placed = (
        ROWS_SPLIT,
        ROWS_SPLIT,
        ROWS_SPLIT,
        ROWS_SPLIT,
        P(),
        P(),
    )
    return jax.shard_map(
        shards,
        mesh=fine_mesh,
        in_specs=placed,
        out_specs=(
            ROWS_SPLIT,
            ROWS_SPLIT,
            ROWS_SPLIT,
            ROWS_SPLIT,
            P(),
            P(),
        ),
        check_vma=False,
    )
```

```python
import jax
import jax.numpy as jnp
from jax import lax
from jax.experimental import pallas as pl
from jax.experimental.pallas import tpu as pltpu
from jax.sharding import Mesh, PartitionSpec as P

H = 12
KVH = 4
GROUP = H // KVH
DH = 128
FH = 64
TOK = 128
N_SEQ = 32
ROWS = H * DH // N_SEQ
PAD = 16
SEQ = ("x", "z")
F32 = jnp.float32
BF16 = jnp.bfloat16


def nn(left, right):
    return lax.dot_general(left, right, (((1,), (0,)), ((), ())), preferred_element_type=F32)


def nt(left, right):
    return lax.dot_general(left, right, (((1,), (1,)), ((), ())), preferred_element_type=F32)


def tn(left, right):
    return lax.dot_general(left, right, (((0,), (0,)), ((), ())), preferred_element_type=F32)


def of_head(h):
    return slice(h * DH, (h + 1) * DH)


def pieces(h):
    row, end = h * DH, (h + 1) * DH
    while row < end:
        block, first = divmod(row, ROWS)
        count = min(ROWS - first, end - row)
        yield block, first, count, row - h * DH
        row += count


def put_head(ref, base, h, rows):
    for block, first, count, start in pieces(h):
        ref[block, base + first : base + first + count, :] = rows[start : start + count]


def get_head(ref, base, h):
    parts = [
        ref[block, base + first : base + first + count, :]
        for block, first, count, start in pieces(h)
    ]
    return jnp.concatenate(parts, axis=0)


def two_softmaxes(scores):
    high = jnp.exp(scores - jnp.max(scores, axis=0, keepdims=True))
    low = jnp.exp(jnp.min(scores, axis=0, keepdims=True) - scores)
    high = high * (1.0 / jnp.sum(high, axis=0, keepdims=True))
    low = low * (1.0 / jnp.sum(low, axis=0, keepdims=True))
    return jnp.concatenate([high, low], axis=0)


def causal():
    shape = (TOK, TOK)
    key = lax.broadcasted_iota(jnp.int32, shape, 0)
    query = lax.broadcasted_iota(jnp.int32, shape, 1)
    return key <= query


def back_through(prob, grad):
    p1, p2 = prob[:FH], prob[FH:]
    d1, d2 = grad[:FH], grad[FH:]
    inner1 = jnp.sum(p1 * d1, axis=0, keepdims=True)
    inner2 = jnp.sum(p2 * d2, axis=0, keepdims=True)
    return (p1 * (d1 - inner1) - p2 * (d2 - inner2)).astype(BF16)


def key_kernel(k_ref, v_ref, km_ref, send_ref, pk_ref, norm_ref):
    ones = jnp.ones((8, TOK), BF16)
    norm_ref[...] = jnp.zeros_like(norm_ref)
    for h in range(H):
        kv = of_head(h // GROUP)
        prob = two_softmaxes(nt(km_ref[h], k_ref[:, kv]))
        pk_ref[h] = prob
        feat = prob.astype(BF16)
        put_head(send_ref, 0, h, nn(feat, v_ref[:, kv]))
        norm_ref[h : h + 1, :] = nt(ones, feat)[0:1]
    send_ref[:, ROWS:, :] = jnp.broadcast_to(norm_ref[...][None], (N_SEQ, PAD, DH))


def query_kernel(q_ref, v_ref, qm_ref, pk_ref, pq_ref, low_ref, rows_ref, num_ref):
    mask = causal()
    rows_ref[...] = jnp.ones_like(rows_ref)
    for h in range(H):
        prob = two_softmaxes(nt(qm_ref[h], q_ref[:, of_head(h)]))
        pq_ref[h] = prob
        scores = jnp.where(mask, tn(pk_ref[h].astype(BF16), prob.astype(BF16)), 0.0)
        low = scores.astype(BF16)
        low_ref[h] = low
        rows_ref[h : h + 1, :] = jnp.sum(scores, axis=0, keepdims=True)
        num_ref[:, of_head(h)] = tn(low, v_ref[:, of_head(h // GROUP)])


def weigh_kernel(
    me_ref, got_ref, pq_ref, rows_ref, g_ref, send_ref, gn_ref, rden_ref, norm_ref
):
    me = me_ref[0]
    state = jnp.zeros((ROWS, DH), F32)
    norm = jnp.zeros((PAD, DH), F32)
    for j in range(N_SEQ):
        send_ref[j, :ROWS, :] = state
        state = state + got_ref[j, :ROWS, :]
        norm = norm + jnp.where(j < me, got_ref[j, ROWS:, :], 0.0)
    norm_ref[...] = norm
    columns = norm.T
    rden_ref[...] = rows_ref[...]
    for h in range(H):
        feat = pq_ref[h].astype(BF16).astype(F32)
        rden_ref[h : h + 1, :] += jnp.sum(feat * columns[:, h : h + 1], axis=0, keepdims=True)
    rden_ref[...] = 1.0 / rden_ref[...]
    scale = rden_ref[...].T
    for h in range(H):
        grad = (g_ref[:, of_head(h)].astype(F32) * scale[:, h : h + 1]).astype(BF16)
        gn_ref[:, of_head(h)] = grad
        put_head(send_ref, ROWS, h, nn(pq_ref[h].astype(BF16), grad))


def finish_kernel(
    got_ref, pq_ref, num_ref, rden_ref, g_ref, att_ref, send_ref, gd_ref, low_ref, col_ref
):
    state = jnp.zeros((ROWS, DH), F32)
    for j in reversed(range(N_SEQ)):
        send_ref[j, :ROWS, :] = state
        state = state + got_ref[j, ROWS:, :]
    scale = rden_ref[...].T
    col_ref[...] = jnp.zeros_like(col_ref)
    for h in range(H):
        low = get_head(got_ref, 0, h).astype(BF16)
        low_ref[h] = low
        out = num_ref[:, of_head(h)] + tn(pq_ref[h].astype(BF16), low)
        out = out * scale[:, h : h + 1]
        att_ref[:, of_head(h)] = out.astype(BF16)
        col_ref[:, h : h + 1] = jnp.sum(g_ref[:, of_head(h)].astype(F32) * out, axis=1, keepdims=True)
    grad = -col_ref[...].T[:PAD] * rden_ref[...]
    gd_ref[...] = grad
    top = grad.astype(BF16)
    rest = grad - top.astype(F32)
    middle = rest.astype(BF16)
    bottom = (rest - middle.astype(F32)).astype(BF16)
    split = jnp.concatenate([top, middle, bottom], axis=0)
    send_ref[:, ROWS:, :] = jnp.zeros((N_SEQ, PAD, DH), F32)
    for h in range(H):
        parts = nt(split, pq_ref[h].astype(BF16))
        norm = parts[h : h + 1] + parts[PAD + h : PAD + h + 1] + parts[2 * PAD + h : 2 * PAD + h + 1]
        send_ref[:, ROWS + h : ROWS + h + 1, :] = jnp.broadcast_to(norm[None], (N_SEQ, 1, DH))


def inner_kernel(
    q_ref, v_ref, qm_ref, pq_ref, pk_ref, low_ref, gn_ref, gd_ref, state_ref, norm_ref,
    qg_ref, qw_ref, part_ref, vpart_ref,
):
    mask = causal()
    columns = norm_ref[...].T
    for kv in range(KVH):
        value = v_ref[:, of_head(kv)]
        value_sum = None
        for h in range(kv * GROUP, (kv + 1) * GROUP):
            prob = pq_ref[h]
            grad = gn_ref[:, of_head(h)]
            den = gd_ref[h : h + 1, :]
            dscore = jnp.where(mask, nt(value, grad) + den, 0.0).astype(BF16)
            grad_feat = nn(pk_ref[h].astype(BF16), dscore) + nt(state_ref[h], grad)
            grad_feat = grad_feat + columns[:, h : h + 1] * den
            grad_u = back_through(prob, grad_feat)
            qw_ref[h] = nn(grad_u, q_ref[:, of_head(h)])
            qg_ref[:, of_head(h)] = tn(grad_u, qm_ref[h]).astype(BF16)
            part_ref[h] = nt(prob.astype(BF16), dscore)
            term = nn(low_ref[h], grad)
            value_sum = term if value_sum is None else value_sum + term
        vpart_ref[:, of_head(kv)] = value_sum


def outer_kernel(
    me_ref, core_ref, got_ref, part_ref, pk_ref, k_ref, v_ref, qw_ref,
    keep_ref, give_ref, gu_ref, low_ref,
):
    me = me_ref[0]
    first = core_ref[0] == 0
    norm = jnp.zeros((PAD, DH), F32)
    for j in range(N_SEQ):
        norm = norm + jnp.where(j > me, got_ref[j, ROWS:, :], 0.0)
    columns = norm.T
    for h in range(H):
        kv = of_head(h // GROUP)
        low = get_head(got_ref, 0, h).astype(BF16)
        low_ref[h] = low
        grad_feat = part_ref[h] + nt(low, v_ref[:, kv]) + columns[:, h : h + 1]
        grad_u = back_through(pk_ref[h], grad_feat)
        gu_ref[h] = grad_u
        key_weight = nn(grad_u, k_ref[:, kv])
        query_weight = qw_ref[h]
        keep_ref[h] = jnp.where(first, query_weight, key_weight)
        give_ref[h] = jnp.where(first, key_weight, query_weight)


def last_kernel(km_ref, pk_ref, gu_ref, low_ref, vpart_ref, kg_ref, vg_ref):
    for kv in range(KVH):
        value_sum = vpart_ref[:, of_head(kv)]
        key_sum = None
        for h in range(kv * GROUP, (kv + 1) * GROUP):
            value_sum = value_sum + tn(pk_ref[h].astype(BF16), low_ref[h])
            term = tn(gu_ref[h], km_ref[h])
            key_sum = term if key_sum is None else key_sum + term
        vg_ref[:, of_head(kv)] = value_sum.astype(BF16)
        kg_ref[:, of_head(kv)] = key_sum.astype(BF16)


def run(kernel, outs, scalars, *arrays, scratch=(), macs=0):
    vmem = pl.BlockSpec(memory_space=pltpu.VMEM)
    smem = pl.BlockSpec(memory_space=pltpu.SMEM)
    moved = sum(a.size * a.dtype.itemsize for a in arrays)
    return pl.pallas_call(
        kernel,
        out_shape=tuple(jax.ShapeDtypeStruct(shape, dtype) for shape, dtype in outs),
        in_specs=[smem] * len(scalars) + [vmem] * len(arrays),
        out_specs=tuple(vmem for _ in outs),
        scratch_shapes=list(scratch),
        cost_estimate=pl.CostEstimate(
            flops=2 * macs * H * DH**3, bytes_accessed=2 * moved, transcendentals=0
        ),
        compiler_params=pltpu.CompilerParams(vmem_limit_bytes=32 * 1024 * 1024),
    )(*scalars, *arrays)


def exchange(blocks, axes):
    return lax.all_to_all(blocks, axes, 0, 0, tiled=True)


def spread(rows, count):
    return jnp.broadcast_to(rows[None], (count,) + rows.shape)


def shards(queries, key_rows, value_rows, out_grad, query_map, key_map):
    q, k, v, g = queries[0], key_rows[0], value_rows[0], out_grad[0]
    qm, km = jnp.swapaxes(query_map, 1, 2), jnp.swapaxes(key_map, 1, 2)
    me = lax.axis_index(SEQ).astype(jnp.int32).reshape(1)
    core = lax.axis_index("core").astype(jnp.int32).reshape(1)
    square = (H, DH, DH)
    wide = (TOK, H * DH)
    narrow = (TOK, KVH * DH)
    half = (H, FH, DH)
    small = (PAD, DH)
    short = (N_SEQ, ROWS + PAD, DH)

    send, pk = run(
        key_kernel, [(short, F32), (square, F32)], (), k, v, km,
        scratch=[pltpu.VMEM(small, F32)], macs=2,
    )
    first = exchange(send, SEQ)
    pq, low, rows, num = run(
        query_kernel, [(square, F32), (square, BF16), (small, F32), (wide, F32)], (), q, v, qm, pk, macs=3
    )
    send, gn, rden, norm = run(
        weigh_kernel,
        [((N_SEQ, 2 * ROWS, DH), F32), (wide, BF16), (small, F32), (small, F32)],
        (me,), first, pq, rows, g, macs=1,
    )
    second = exchange(send, SEQ)
    attended, send, gd, state = run(
        finish_kernel,
        [(wide, BF16), (short, F32), (small, F32), (square, BF16)],
        (), second, pq, num, rden, g, scratch=[pltpu.VMEM((TOK, DH), F32)], macs=1,
    )
    third = exchange(send, SEQ)
    query_grad, query_weight, part, value_part = run(
        inner_kernel,
        [(wide, BF16), (half, F32), (square, F32), (narrow, F32)],
        (), q, v, qm, pq, pk, low, gn, gd, state, norm, macs=7,
    )
    keep, give, grad_u, back = run(
        outer_kernel,
        [(half, F32), (half, F32), (half, BF16), (square, BF16)],
        (me, core), third, part, pk, k, v, query_weight, macs=2,
    )
    swap = [(0, 1), (1, 0)]
    mine = keep + lax.ppermute(give, "core", swap)
    mine = exchange(mine.reshape(16, ROWS, DH), ("y", "x")).sum(0)
    mine = exchange(spread(mine, 8), "z").sum(0)
    mine = exchange(spread(mine, 16), ("y", "x")).reshape(half)
    key_grad, value_grad = run(
        last_kernel, [(narrow, BF16), (narrow, BF16)], (), km, pk, grad_u, back, value_part, macs=2
    )
    other = lax.ppermute(mine, "core", swap)
    query_total = jnp.where(core[0] == 0, mine, other)
    key_total = jnp.where(core[0] == 0, other, mine)
    return (
        attended[None],
        query_grad[None],
        key_grad[None],
        value_grad[None],
        jnp.swapaxes(query_total, 1, 2),
        jnp.swapaxes(key_total, 1, 2),
    )


ROWS_SPLIT = P(("y", "core"), ("x", "z"), None)


def solution(mesh):
    fine_mesh = Mesh(mesh.devices.reshape(4, 2, 4, 8), ("y", "core", "x", "z"))
    placed = (ROWS_SPLIT, ROWS_SPLIT, ROWS_SPLIT, ROWS_SPLIT, P(), P())
    return jax.shard_map(
        shards,
        mesh=fine_mesh,
        in_specs=placed,
        out_specs=placed,
        check_vma=False,
    )
```

```python
import jax
import jax.numpy as jnp
from jax import lax
from jax.experimental import pallas as pl
from jax.experimental.pallas import tpu as pltpu
from jax.sharding import Mesh, PartitionSpec as P

H = 12
KVH = 4
GROUP = H // KVH
DH = 128
FH = 64
TOK = 128
NX = 4
NZ = 8
ROWS = H * DH // NZ
PAD = 16
RING = (0, 1, 3, 5, 7, 6, 4, 2)
SLOT = [RING.index(place) for place in range(NZ)]
F32 = jnp.float32
BF16 = jnp.bfloat16


def nn(left, right):
    return lax.dot_general(left, right, (((1,), (0,)), ((), ())), preferred_element_type=F32)


def nt(left, right):
    return lax.dot_general(left, right, (((1,), (1,)), ((), ())), preferred_element_type=F32)


def tn(left, right):
    return lax.dot_general(left, right, (((0,), (0,)), ((), ())), preferred_element_type=F32)


def of_head(h):
    return slice(h * DH, (h + 1) * DH)


def pieces(h):
    row, end = h * DH, (h + 1) * DH
    while row < end:
        block, first = divmod(row, ROWS)
        count = min(ROWS - first, end - row)
        yield block, first, count, row - h * DH
        row += count


def put_head(ref, base, h, rows):
    for block, first, count, start in pieces(h):
        ref[SLOT[block], base + first : base + first + count, :] = rows[start : start + count]


def get_head(ref, base, h):
    parts = [
        ref[SLOT[block], base + first : base + first + count, :]
        for block, first, count, start in pieces(h)
    ]
    return jnp.concatenate(parts, axis=0)


def two_softmaxes(scores):
    high = jnp.exp(scores - jnp.max(scores, axis=0, keepdims=True))
    low = jnp.exp(jnp.min(scores, axis=0, keepdims=True) - scores)
    high = high * (1.0 / jnp.sum(high, axis=0, keepdims=True))
    low = low * (1.0 / jnp.sum(low, axis=0, keepdims=True))
    return jnp.concatenate([high, low], axis=0)


def causal():
    shape = (TOK, TOK)
    key = lax.broadcasted_iota(jnp.int32, shape, 0)
    query = lax.broadcasted_iota(jnp.int32, shape, 1)
    return key <= query


def back_through(prob, grad):
    p1, p2 = prob[:FH], prob[FH:]
    d1, d2 = grad[:FH], grad[FH:]
    inner1 = jnp.sum(p1 * d1, axis=0, keepdims=True)
    inner2 = jnp.sum(p2 * d2, axis=0, keepdims=True)
    return (p1 * (d1 - inner1) - p2 * (d2 - inner2)).astype(BF16)


def key_kernel(k_ref, v_ref, km_ref, send_ref, pk_ref, norm_ref):
    ones = jnp.ones((8, TOK), BF16)
    norm_ref[...] = jnp.zeros_like(norm_ref)
    for h in range(H):
        kv = of_head(h // GROUP)
        prob = two_softmaxes(nt(km_ref[h], k_ref[:, kv]))
        pk_ref[h] = prob
        feat = prob.astype(BF16)
        put_head(send_ref, 0, h, nn(feat, v_ref[:, kv]))
        norm_ref[h : h + 1, :] = nt(ones, feat)[0:1]
    send_ref[:, ROWS:, :] = jnp.broadcast_to(norm_ref[...][None], (NZ, PAD, DH))


def query_kernel(q_ref, v_ref, qm_ref, pk_ref, pq_ref, low_ref, rows_ref, num_ref):
    mask = causal()
    rows_ref[...] = jnp.ones_like(rows_ref)
    for h in range(H):
        prob = two_softmaxes(nt(qm_ref[h], q_ref[:, of_head(h)]))
        pq_ref[h] = prob
        scores = jnp.where(mask, tn(pk_ref[h].astype(BF16), prob.astype(BF16)), 0.0)
        low = scores.astype(BF16)
        low_ref[h] = low
        rows_ref[h : h + 1, :] = jnp.sum(scores, axis=0, keepdims=True)
        num_ref[:, of_head(h)] = tn(low, v_ref[:, of_head(h // GROUP)])


def total_kernel(got_ref, out_ref):
    total = got_ref[0]
    for j in range(1, NZ):
        total = total + got_ref[j]
    out_ref[...] = total


def from_rows(x, one_ref, two_ref, three_ref, rows, earlier):
    total = jnp.zeros((rows.stop - rows.start, DH), F32)
    for step, ref in ((1, one_ref), (2, two_ref), (3, three_ref)):
        wanted = x >= step if earlier else x < step
        total = total + jnp.where(wanted, ref[rows, :], 0.0)
    return total


STATE = slice(0, ROWS)
NORM = slice(ROWS, ROWS + PAD)


def weigh_kernel(
    x_ref, z_ref, got_ref, one_ref, two_ref, three_ref, pq_ref, rows_ref, g_ref,
    send_ref, gn_ref, rden_ref, norm_ref,
):
    x, z = x_ref[0], z_ref[0]
    state = from_rows(x, one_ref, two_ref, three_ref, STATE, True)
    norm = from_rows(x, one_ref, two_ref, three_ref, NORM, True)
    for j in range(NZ):
        send_ref[SLOT[j], STATE, :] = state
        if j < NZ - 1:
            state = state + got_ref[SLOT[j], STATE, :]
            norm = norm + jnp.where(j < z, got_ref[SLOT[j], NORM, :], 0.0)
    norm_ref[...] = norm
    columns = norm.T
    rden_ref[...] = rows_ref[...]
    for h in range(H):
        feat = pq_ref[h].astype(BF16).astype(F32)
        rden_ref[h : h + 1, :] += jnp.sum(feat * columns[:, h : h + 1], axis=0, keepdims=True)
    rden_ref[...] = 1.0 / rden_ref[...]
    scale = rden_ref[...].T
    for h in range(H):
        grad = (g_ref[:, of_head(h)].astype(F32) * scale[:, h : h + 1]).astype(BF16)
        gn_ref[:, of_head(h)] = grad
        put_head(send_ref, ROWS, h, nn(pq_ref[h].astype(BF16), grad))


def finish_kernel(
    got_ref, pq_ref, num_ref, rden_ref, g_ref, att_ref, sum_ref, gd_ref, low_ref, col_ref
):
    total = got_ref[0, ROWS:, :]
    for j in range(1, NZ):
        total = total + got_ref[j, ROWS:, :]
    sum_ref[STATE, :] = total
    scale = rden_ref[...].T
    col_ref[...] = jnp.zeros_like(col_ref)
    for h in range(H):
        low = get_head(got_ref, 0, h).astype(BF16)
        low_ref[h] = low
        out = num_ref[:, of_head(h)] + tn(pq_ref[h].astype(BF16), low)
        out = out * scale[:, h : h + 1]
        att_ref[:, of_head(h)] = out.astype(BF16)
        col_ref[:, h : h + 1] = jnp.sum(g_ref[:, of_head(h)].astype(F32) * out, axis=1, keepdims=True)
    grad = -col_ref[...].T[:PAD] * rden_ref[...]
    gd_ref[...] = grad
    top = grad.astype(BF16)
    rest = grad - top.astype(F32)
    middle = rest.astype(BF16)
    bottom = (rest - middle.astype(F32)).astype(BF16)
    split = jnp.concatenate([top, middle, bottom], axis=0)
    sum_ref[NORM, :] = jnp.zeros((PAD, DH), F32)
    for h in range(H):
        parts = nt(split, pq_ref[h].astype(BF16))
        norm = parts[h : h + 1] + parts[PAD + h : PAD + h + 1] + parts[2 * PAD + h : 2 * PAD + h + 1]
        sum_ref[ROWS + h : ROWS + h + 1, :] = norm


def suffix_kernel(x_ref, z_ref, got_ref, own_ref, one_ref, two_ref, three_ref, send_ref):
    x, z = x_ref[0], z_ref[0]
    state = from_rows(x, one_ref, two_ref, three_ref, STATE, False)
    norm = from_rows(x, one_ref, two_ref, three_ref, NORM, False)
    both = norm + own_ref[NORM, :]
    for j in reversed(range(NZ)):
        send_ref[SLOT[j], STATE, :] = state
        send_ref[SLOT[j], NORM, :] = jnp.where(z > j, both, norm)
        if j > 0:
            state = state + got_ref[SLOT[j], ROWS:, :]


def inner_kernel(
    q_ref, v_ref, qm_ref, pq_ref, pk_ref, low_ref, gn_ref, gd_ref, state_ref, norm_ref,
    qg_ref, qw_ref, part_ref, vpart_ref,
):
    mask = causal()
    columns = norm_ref[...].T
    for kv in range(KVH):
        value = v_ref[:, of_head(kv)]
        value_sum = None
        for h in range(kv * GROUP, (kv + 1) * GROUP):
            prob = pq_ref[h]
            grad = gn_ref[:, of_head(h)]
            den = gd_ref[h : h + 1, :]
            dscore = jnp.where(mask, nt(value, grad) + den, 0.0).astype(BF16)
            grad_feat = nn(pk_ref[h].astype(BF16), dscore) + nt(state_ref[h], grad)
            grad_feat = grad_feat + columns[:, h : h + 1] * den
            grad_u = back_through(prob, grad_feat)
            qw_ref[h] = nn(grad_u, q_ref[:, of_head(h)])
            qg_ref[:, of_head(h)] = tn(grad_u, qm_ref[h]).astype(BF16)
            part_ref[h] = nt(prob.astype(BF16), dscore)
            term = nn(low_ref[h], grad)
            value_sum = term if value_sum is None else value_sum + term
        vpart_ref[:, of_head(kv)] = value_sum


def outer_kernel(
    core_ref, got_ref, part_ref, pk_ref, k_ref, v_ref, qw_ref,
    keep_ref, give_ref, gu_ref, low_ref,
):
    first = core_ref[0] == 0
    norm = got_ref[0, NORM, :]
    for j in range(1, NZ):
        norm = norm + got_ref[j, NORM, :]
    columns = norm.T
    for h in range(H):
        kv = of_head(h // GROUP)
        low = get_head(got_ref, 0, h).astype(BF16)
        low_ref[h] = low
        grad_feat = part_ref[h] + nt(low, v_ref[:, kv]) + columns[:, h : h + 1]
        grad_u = back_through(pk_ref[h], grad_feat)
        gu_ref[h] = grad_u
        key_weight = nn(grad_u, k_ref[:, kv])
        query_weight = qw_ref[h]
        keep_ref[h] = jnp.where(first, query_weight, key_weight)
        give_ref[h] = jnp.where(first, key_weight, query_weight)


def last_kernel(km_ref, pk_ref, gu_ref, low_ref, vpart_ref, kg_ref, vg_ref):
    for kv in range(KVH):
        value_sum = vpart_ref[:, of_head(kv)]
        key_sum = None
        for h in range(kv * GROUP, (kv + 1) * GROUP):
            value_sum = value_sum + tn(pk_ref[h].astype(BF16), low_ref[h])
            term = tn(gu_ref[h], km_ref[h])
            key_sum = term if key_sum is None else key_sum + term
        vg_ref[:, of_head(kv)] = value_sum.astype(BF16)
        kg_ref[:, of_head(kv)] = key_sum.astype(BF16)


def run(kernel, outs, scalars, *arrays, scratch=(), macs=0):
    vmem = pl.BlockSpec(memory_space=pltpu.VMEM)
    smem = pl.BlockSpec(memory_space=pltpu.SMEM)
    moved = sum(a.size * a.dtype.itemsize for a in arrays)
    return pl.pallas_call(
        kernel,
        out_shape=tuple(jax.ShapeDtypeStruct(shape, dtype) for shape, dtype in outs),
        in_specs=[smem] * len(scalars) + [vmem] * len(arrays),
        out_specs=tuple(vmem for _ in outs),
        scratch_shapes=list(scratch),
        cost_estimate=pl.CostEstimate(
            flops=2 * macs * H * DH**3, bytes_accessed=2 * moved, transcendentals=0
        ),
        compiler_params=pltpu.CompilerParams(vmem_limit_bytes=32 * 1024 * 1024),
    )(*scalars, *arrays)


def exchange(blocks, axes):
    return lax.all_to_all(blocks, axes, 0, 0, tiled=True)


def turn(rows):
    return [lax.ppermute(rows, "x", [(i, (i + step) % NX) for i in range(NX)]) for step in (1, 2, 3)]


def exchange_z(blocks):
    return lax.all_to_all(blocks, "z", 0, 0, axis_index_groups=[list(RING)], tiled=True)


def spread(rows, count):
    return jnp.broadcast_to(rows[None], (count,) + rows.shape)


def shards(queries, key_rows, value_rows, out_grad, query_map, key_map):
    q, k, v, g = queries[0], key_rows[0], value_rows[0], out_grad[0]
    qm, km = jnp.swapaxes(query_map, 1, 2), jnp.swapaxes(key_map, 1, 2)
    x, z, core = (lax.axis_index(a).astype(jnp.int32).reshape(1) for a in ("x", "z", "core"))
    square = (H, DH, DH)
    wide = (TOK, H * DH)
    narrow = (TOK, KVH * DH)
    half = (H, FH, DH)
    small = (PAD, DH)
    flat = (ROWS + PAD, DH)
    short = (NZ,) + flat

    send, pk = run(
        key_kernel, [(short, F32), (square, F32)], (), k, v, km,
        scratch=[pltpu.VMEM(small, F32)], macs=2,
    )
    first = exchange_z(send)
    (total,) = run(total_kernel, [(flat, F32)], (), first)
    others = turn(total)
    pq, low, rows, num = run(
        query_kernel, [(square, F32), (square, BF16), (small, F32), (wide, F32)], (), q, v, qm, pk, macs=3
    )
    send, gn, rden, norm = run(
        weigh_kernel,
        [((NZ, 2 * ROWS, DH), F32), (wide, BF16), (small, F32), (small, F32)],
        (x, z), first, *others, pq, rows, g, macs=1,
    )
    second = exchange_z(send)
    attended, total, gd, state = run(
        finish_kernel,
        [(wide, BF16), (flat, F32), (small, F32), (square, BF16)],
        (), second, pq, num, rden, g, scratch=[pltpu.VMEM((TOK, DH), F32)], macs=1,
    )
    others = turn(total)
    (send,) = run(suffix_kernel, [(short, F32)], (x, z), second, total, *others)
    third = exchange_z(send)
    query_grad, query_weight, part, value_part = run(
        inner_kernel,
        [(wide, BF16), (half, F32), (square, F32), (narrow, F32)],
        (), q, v, qm, pq, pk, low, gn, gd, state, norm, macs=7,
    )
    keep, give, grad_u, back = run(
        outer_kernel,
        [(half, F32), (half, F32), (half, BF16), (square, BF16)],
        (core,), third, part, pk, k, v, query_weight, macs=2,
    )
    swap = [(0, 1), (1, 0)]
    mine = keep + lax.ppermute(give, "core", swap)
    mine = exchange(mine.reshape(16, -1, DH), ("y", "x")).sum(0)
    mine = exchange_z(spread(mine, 8)).sum(0)
    mine = exchange(spread(mine, 16), ("y", "x")).reshape(half)
    key_grad, value_grad = run(
        last_kernel, [(narrow, BF16), (narrow, BF16)], (), km, pk, grad_u, back, value_part, macs=2
    )
    other = lax.ppermute(mine, "core", swap)
    query_total = jnp.where(core[0] == 0, mine, other)
    key_total = jnp.where(core[0] == 0, other, mine)
    return (
        attended[None],
        query_grad[None],
        key_grad[None],
        value_grad[None],
        jnp.swapaxes(query_total, 1, 2),
        jnp.swapaxes(key_total, 1, 2),
    )


ROWS_SPLIT = P(("y", "core"), ("x", "z"), None)


def solution(mesh):
    fine_mesh = Mesh(mesh.devices.reshape(4, 2, 4, 8), ("y", "core", "x", "z"))
    placed = (ROWS_SPLIT, ROWS_SPLIT, ROWS_SPLIT, ROWS_SPLIT, P(), P())
    return jax.shard_map(
        shards,
        mesh=fine_mesh,
        in_specs=placed,
        out_specs=placed,
        check_vma=False,
    )
```

```python
import jax
import jax.numpy as jnp
from jax import lax
from jax.experimental import pallas as pl
from jax.experimental.pallas import tpu as pltpu
from jax.sharding import Mesh, PartitionSpec as P

H = 12
KVH = 4
GROUP = H // KVH
DH = 128
FH = 64
TOK = 128
NX = 4
NZ = 8
ROWS = H * DH // NZ
PAD = 16
RING = (0, 1, 3, 5, 7, 6, 4, 2)
SLOT = [RING.index(place) for place in range(NZ)]
F32 = jnp.float32
BF16 = jnp.bfloat16


def nn(left, right):
    return lax.dot_general(left, right, (((1,), (0,)), ((), ())), preferred_element_type=F32)


def nt(left, right):
    return lax.dot_general(left, right, (((1,), (1,)), ((), ())), preferred_element_type=F32)


def tn(left, right):
    return lax.dot_general(left, right, (((0,), (0,)), ((), ())), preferred_element_type=F32)


def of_head(h):
    return slice(h * DH, (h + 1) * DH)


def pieces(h):
    row, end = h * DH, (h + 1) * DH
    while row < end:
        block, first = divmod(row, ROWS)
        count = min(ROWS - first, end - row)
        yield block, first, count, row - h * DH
        row += count


def put_head(ref, base, h, rows):
    for block, first, count, start in pieces(h):
        ref[SLOT[block], base + first : base + first + count, :] = rows[start : start + count]


def get_head(ref, base, h):
    parts = [
        ref[SLOT[block], base + first : base + first + count, :]
        for block, first, count, start in pieces(h)
    ]
    return jnp.concatenate(parts, axis=0)


def two_softmaxes(scores):
    high = jnp.exp(scores - jnp.max(scores, axis=0, keepdims=True))
    low = jnp.exp(jnp.min(scores, axis=0, keepdims=True) - scores)
    high = high * (1.0 / jnp.sum(high, axis=0, keepdims=True))
    low = low * (1.0 / jnp.sum(low, axis=0, keepdims=True))
    return jnp.concatenate([high, low], axis=0)


def causal():
    shape = (TOK, TOK)
    key = lax.broadcasted_iota(jnp.int32, shape, 0)
    query = lax.broadcasted_iota(jnp.int32, shape, 1)
    return key <= query


def back_through(prob, grad):
    p1, p2 = prob[:FH], prob[FH:]
    d1, d2 = grad[:FH], grad[FH:]
    inner1 = jnp.sum(p1 * d1, axis=0, keepdims=True)
    inner2 = jnp.sum(p2 * d2, axis=0, keepdims=True)
    return (p1 * (d1 - inner1) - p2 * (d2 - inner2)).astype(BF16)


def key_kernel(k_ref, v_ref, km_ref, send_ref, pk_ref, norm_ref):
    ones = jnp.ones((8, TOK), BF16)
    norm_ref[...] = jnp.zeros_like(norm_ref)
    for h in range(H):
        kv = of_head(h // GROUP)
        prob = two_softmaxes(nt(km_ref[h], k_ref[:, kv]))
        pk_ref[h] = prob
        feat = prob.astype(BF16)
        put_head(send_ref, 0, h, nn(feat, v_ref[:, kv]))
        norm_ref[h : h + 1, :] = nt(ones, feat)[0:1]
    send_ref[:, ROWS:, :] = jnp.broadcast_to(norm_ref[...][None], (NZ, PAD, DH))


def query_kernel(q_ref, v_ref, qm_ref, pk_ref, pq_ref, low_ref, rows_ref, num_ref):
    mask = causal()
    rows_ref[...] = jnp.ones_like(rows_ref)
    for h in range(H):
        prob = two_softmaxes(nt(qm_ref[h], q_ref[:, of_head(h)]))
        pq_ref[h] = prob
        scores = jnp.where(mask, tn(pk_ref[h].astype(BF16), prob.astype(BF16)), 0.0)
        low = scores.astype(BF16)
        low_ref[h] = low
        rows_ref[h : h + 1, :] = jnp.sum(scores, axis=0, keepdims=True)
        num_ref[:, of_head(h)] = tn(low, v_ref[:, of_head(h // GROUP)])


def total_kernel(got_ref, out_ref):
    total = got_ref[0]
    for j in range(1, NZ):
        total = total + got_ref[j]
    out_ref[...] = total


def from_rows(x, one_ref, two_ref, three_ref, rows, earlier):
    total = jnp.zeros((rows.stop - rows.start, DH), F32)
    for step, ref in ((1, one_ref), (2, two_ref), (3, three_ref)):
        wanted = x >= step if earlier else x < step
        total = total + jnp.where(wanted, ref[rows, :], 0.0)
    return total


STATE = slice(0, ROWS)
NORM = slice(ROWS, ROWS + PAD)


def weigh_kernel(
    x_ref, z_ref, got_ref, one_ref, two_ref, three_ref, pq_ref, rows_ref, g_ref,
    send_ref, gn_ref, rden_ref, norm_ref,
):
    x, z = x_ref[0], z_ref[0]
    state = from_rows(x, one_ref, two_ref, three_ref, STATE, True)
    norm = from_rows(x, one_ref, two_ref, three_ref, NORM, True)
    for j in range(NZ):
        send_ref[SLOT[j], STATE, :] = state
        if j < NZ - 1:
            state = state + got_ref[SLOT[j], STATE, :]
            norm = norm + jnp.where(j < z, got_ref[SLOT[j], NORM, :], 0.0)
    norm_ref[...] = norm
    columns = norm.T
    rden_ref[...] = rows_ref[...]
    for h in range(H):
        feat = pq_ref[h].astype(BF16).astype(F32)
        rden_ref[h : h + 1, :] += jnp.sum(feat * columns[:, h : h + 1], axis=0, keepdims=True)
    rden_ref[...] = 1.0 / rden_ref[...]
    scale = rden_ref[...].T
    for h in range(H):
        grad = (g_ref[:, of_head(h)].astype(F32) * scale[:, h : h + 1]).astype(BF16)
        gn_ref[:, of_head(h)] = grad
        put_head(send_ref, ROWS, h, nn(pq_ref[h].astype(BF16), grad))


def finish_kernel(
    got_ref, pq_ref, num_ref, rden_ref, g_ref, att_ref, sum_ref, gd_ref, low_ref, col_ref
):
    total = got_ref[0, ROWS:, :]
    for j in range(1, NZ):
        total = total + got_ref[j, ROWS:, :]
    sum_ref[STATE, :] = total
    scale = rden_ref[...].T
    col_ref[...] = jnp.zeros_like(col_ref)
    for h in range(H):
        low = get_head(got_ref, 0, h).astype(BF16)
        low_ref[h] = low
        out = num_ref[:, of_head(h)] + tn(pq_ref[h].astype(BF16), low)
        out = out * scale[:, h : h + 1]
        att_ref[:, of_head(h)] = out.astype(BF16)
        col_ref[:, h : h + 1] = jnp.sum(g_ref[:, of_head(h)].astype(F32) * out, axis=1, keepdims=True)
    grad = -col_ref[...].T[:PAD] * rden_ref[...]
    gd_ref[...] = grad
    top = grad.astype(BF16)
    rest = grad - top.astype(F32)
    middle = rest.astype(BF16)
    bottom = (rest - middle.astype(F32)).astype(BF16)
    split = jnp.concatenate([top, middle, bottom], axis=0)
    sum_ref[NORM, :] = jnp.zeros((PAD, DH), F32)
    for h in range(H):
        parts = nt(split, pq_ref[h].astype(BF16))
        norm = parts[h : h + 1] + parts[PAD + h : PAD + h + 1] + parts[2 * PAD + h : 2 * PAD + h + 1]
        sum_ref[ROWS + h : ROWS + h + 1, :] = norm


def suffix_kernel(x_ref, z_ref, got_ref, own_ref, one_ref, two_ref, three_ref, send_ref):
    x, z = x_ref[0], z_ref[0]
    state = from_rows(x, one_ref, two_ref, three_ref, STATE, False)
    norm = from_rows(x, one_ref, two_ref, three_ref, NORM, False)
    both = norm + own_ref[NORM, :]
    for j in reversed(range(NZ)):
        send_ref[SLOT[j], STATE, :] = state
        send_ref[SLOT[j], NORM, :] = jnp.where(z > j, both, norm)
        if j > 0:
            state = state + got_ref[SLOT[j], ROWS:, :]


def inner_kernel(
    q_ref, v_ref, qm_ref, pq_ref, pk_ref, low_ref, gn_ref, gd_ref, state_ref, norm_ref,
    qg_ref, qw_ref, part_ref, vpart_ref,
):
    mask = causal()
    columns = norm_ref[...].T
    for kv in range(KVH):
        value = v_ref[:, of_head(kv)]
        value_sum = None
        for h in range(kv * GROUP, (kv + 1) * GROUP):
            prob = pq_ref[h]
            grad = gn_ref[:, of_head(h)]
            den = gd_ref[h : h + 1, :]
            dscore = jnp.where(mask, nt(value, grad) + den, 0.0).astype(BF16)
            grad_feat = nn(pk_ref[h].astype(BF16), dscore) + nt(state_ref[h], grad)
            grad_feat = grad_feat + columns[:, h : h + 1] * den
            grad_u = back_through(prob, grad_feat)
            qw_ref[h] = nn(grad_u, q_ref[:, of_head(h)])
            qg_ref[:, of_head(h)] = tn(grad_u, qm_ref[h]).astype(BF16)
            part_ref[h] = nt(prob.astype(BF16), dscore)
            term = nn(low_ref[h], grad)
            value_sum = term if value_sum is None else value_sum + term
        vpart_ref[:, of_head(kv)] = value_sum


def outer_kernel(
    core_ref, got_ref, part_ref, pk_ref, k_ref, v_ref, qw_ref,
    keep_ref, give_ref, gu_ref, low_ref,
):
    first = core_ref[0] == 0
    norm = got_ref[0, NORM, :]
    for j in range(1, NZ):
        norm = norm + got_ref[j, NORM, :]
    columns = norm.T
    for h in range(H):
        kv = of_head(h // GROUP)
        low = get_head(got_ref, 0, h).astype(BF16)
        low_ref[h] = low
        grad_feat = part_ref[h] + nt(low, v_ref[:, kv]) + columns[:, h : h + 1]
        grad_u = back_through(pk_ref[h], grad_feat)
        gu_ref[h] = grad_u
        key_weight = nn(grad_u, k_ref[:, kv])
        query_weight = qw_ref[h]
        keep_ref[h] = jnp.where(first, query_weight, key_weight)
        give_ref[h] = jnp.where(first, key_weight, query_weight)


def last_kernel(km_ref, pk_ref, gu_ref, low_ref, vpart_ref, kg_ref, vg_ref):
    for kv in range(KVH):
        value_sum = vpart_ref[:, of_head(kv)]
        key_sum = None
        for h in range(kv * GROUP, (kv + 1) * GROUP):
            value_sum = value_sum + tn(pk_ref[h].astype(BF16), low_ref[h])
            term = tn(gu_ref[h], km_ref[h])
            key_sum = term if key_sum is None else key_sum + term
        vg_ref[:, of_head(kv)] = value_sum.astype(BF16)
        kg_ref[:, of_head(kv)] = key_sum.astype(BF16)


def run(kernel, outs, scalars, *arrays, scratch=(), macs=0):
    vmem = pl.BlockSpec(memory_space=pltpu.VMEM)
    smem = pl.BlockSpec(memory_space=pltpu.SMEM)
    moved = sum(a.size * a.dtype.itemsize for a in arrays)
    return pl.pallas_call(
        kernel,
        out_shape=tuple(jax.ShapeDtypeStruct(shape, dtype) for shape, dtype in outs),
        in_specs=[smem] * len(scalars) + [vmem] * len(arrays),
        out_specs=tuple(vmem for _ in outs),
        scratch_shapes=list(scratch),
        cost_estimate=pl.CostEstimate(
            flops=2 * macs * H * DH**3, bytes_accessed=2 * moved, transcendentals=0
        ),
        compiler_params=pltpu.CompilerParams(vmem_limit_bytes=32 * 1024 * 1024),
    )(*scalars, *arrays)


def exchange(blocks, axes):
    return lax.all_to_all(blocks, axes, 0, 0, tiled=True)


def turn(rows):
    return [lax.ppermute(rows, "x", [(i, (i + step) % NX) for i in range(NX)]) for step in (1, 2, 3)]


def exchange_z(blocks):
    return lax.all_to_all(blocks, "z", 0, 0, axis_index_groups=[list(RING)], tiled=True)


def exchange_after(blocks, token):
    return exchange_z(lax.dynamic_update_slice(blocks, token, (0, ROWS + H, 0)))


def spread(rows, count):
    return jnp.broadcast_to(rows[None], (count,) + rows.shape)


def shards(queries, key_rows, value_rows, out_grad, query_map, key_map):
    q, k, v, g = queries[0], key_rows[0], value_rows[0], out_grad[0]
    qm, km = jnp.swapaxes(query_map, 1, 2), jnp.swapaxes(key_map, 1, 2)
    x, z, core = (lax.axis_index(a).astype(jnp.int32).reshape(1) for a in ("x", "z", "core"))
    square = (H, DH, DH)
    wide = (TOK, H * DH)
    narrow = (TOK, KVH * DH)
    half = (H, FH, DH)
    small = (PAD, DH)
    flat = (ROWS + PAD, DH)
    short = (NZ,) + flat

    send, pk = run(
        key_kernel, [(short, F32), (square, F32)], (), k, v, km,
        scratch=[pltpu.VMEM(small, F32)], macs=2,
    )
    first = lax.cond(core[0] == 0, exchange_z, lambda blocks: blocks, send)
    token = lax.ppermute(first[:1, ROWS + H :, :], "core", [(0, 1)])
    first = lax.cond(core[0] == 0, lambda blocks, token: blocks, exchange_after, first, token)
    (total,) = run(total_kernel, [(flat, F32)], (), first)
    others = turn(total)
    pq, low, rows, num = run(
        query_kernel, [(square, F32), (square, BF16), (small, F32), (wide, F32)], (), q, v, qm, pk, macs=3
    )
    send, gn, rden, norm = run(
        weigh_kernel,
        [((NZ, 2 * ROWS, DH), F32), (wide, BF16), (small, F32), (small, F32)],
        (x, z), first, *others, pq, rows, g, macs=1,
    )
    second = exchange_z(send)
    attended, total, gd, state = run(
        finish_kernel,
        [(wide, BF16), (flat, F32), (small, F32), (square, BF16)],
        (), second, pq, num, rden, g, scratch=[pltpu.VMEM((TOK, DH), F32)], macs=1,
    )
    others = turn(total)
    (send,) = run(suffix_kernel, [(short, F32)], (x, z), second, total, *others)
    third = exchange_z(send)
    query_grad, query_weight, part, value_part = run(
        inner_kernel,
        [(wide, BF16), (half, F32), (square, F32), (narrow, F32)],
        (), q, v, qm, pq, pk, low, gn, gd, state, norm, macs=7,
    )
    keep, give, grad_u, back = run(
        outer_kernel,
        [(half, F32), (half, F32), (half, BF16), (square, BF16)],
        (core,), third, part, pk, k, v, query_weight, macs=2,
    )
    swap = [(0, 1), (1, 0)]
    mine = keep + lax.ppermute(give, "core", swap)
    mine = exchange(mine.reshape(16, -1, DH), ("y", "x")).sum(0)
    mine = exchange_z(spread(mine, 8)).sum(0)
    mine = exchange(spread(mine, 16), ("y", "x")).reshape(half)
    key_grad, value_grad = run(
        last_kernel, [(narrow, BF16), (narrow, BF16)], (), km, pk, grad_u, back, value_part, macs=2
    )
    other = lax.ppermute(mine, "core", swap)
    query_total = jnp.where(core[0] == 0, mine, other)
    key_total = jnp.where(core[0] == 0, other, mine)
    return (
        attended[None],
        query_grad[None],
        key_grad[None],
        value_grad[None],
        jnp.swapaxes(query_total, 1, 2),
        jnp.swapaxes(key_total, 1, 2),
    )


ROWS_SPLIT = P(("y", "core"), ("x", "z"), None)


def solution(mesh):
    fine_mesh = Mesh(mesh.devices.reshape(4, 2, 4, 8), ("y", "core", "x", "z"))
    placed = (ROWS_SPLIT, ROWS_SPLIT, ROWS_SPLIT, ROWS_SPLIT, P(), P())
    return jax.shard_map(
        shards,
        mesh=fine_mesh,
        in_specs=placed,
        out_specs=placed,
        check_vma=False,
    )
```

```python
import jax
import jax.numpy as jnp
from jax import lax
from jax.experimental import pallas as pl
from jax.experimental.pallas import tpu as pltpu
from jax.sharding import Mesh, PartitionSpec as P

H = 12
KVH = 4
GROUP = H // KVH
DH = 128
FH = 64
TOK = 128
NX = 4
NZ = 8
ROWS = H * DH // NZ
PAD = 16
RING = (0, 1, 3, 5, 7, 6, 4, 2)
SLOT = [RING.index(place) for place in range(NZ)]
F32 = jnp.float32
BF16 = jnp.bfloat16


def nn(left, right):
    return lax.dot_general(left, right, (((1,), (0,)), ((), ())), preferred_element_type=F32)


def nt(left, right):
    return lax.dot_general(left, right, (((1,), (1,)), ((), ())), preferred_element_type=F32)


def tn(left, right):
    return lax.dot_general(left, right, (((0,), (0,)), ((), ())), preferred_element_type=F32)


def of_head(h):
    return slice(h * DH, (h + 1) * DH)


def pieces(h):
    row, end = h * DH, (h + 1) * DH
    while row < end:
        block, first = divmod(row, ROWS)
        count = min(ROWS - first, end - row)
        yield block, first, count, row - h * DH
        row += count


def put_head(ref, base, h, rows):
    for block, first, count, start in pieces(h):
        ref[SLOT[block], base + first : base + first + count, :] = rows[start : start + count]


def get_head(ref, base, h):
    parts = [
        ref[SLOT[block], base + first : base + first + count, :]
        for block, first, count, start in pieces(h)
    ]
    return jnp.concatenate(parts, axis=0)


def two_softmaxes(scores):
    high = jnp.exp(scores - jnp.max(scores, axis=0, keepdims=True))
    low = jnp.exp(jnp.min(scores, axis=0, keepdims=True) - scores)
    high = high * (1.0 / jnp.sum(high, axis=0, keepdims=True))
    low = low * (1.0 / jnp.sum(low, axis=0, keepdims=True))
    return jnp.concatenate([high, low], axis=0)


def causal():
    shape = (TOK, TOK)
    key = lax.broadcasted_iota(jnp.int32, shape, 0)
    query = lax.broadcasted_iota(jnp.int32, shape, 1)
    return key <= query


def back_through(prob, grad):
    p1, p2 = prob[:FH], prob[FH:]
    d1, d2 = grad[:FH], grad[FH:]
    inner1 = jnp.sum(p1 * d1, axis=0, keepdims=True)
    inner2 = jnp.sum(p2 * d2, axis=0, keepdims=True)
    return (p1 * (d1 - inner1) - p2 * (d2 - inner2)).astype(BF16)


def key_kernel(k_ref, km_ref, pk_ref):
    for h in range(H):
        pk_ref[h] = two_softmaxes(nt(km_ref[h], k_ref[:, of_head(h // GROUP)]))


def state_kernel(pk_ref, v_ref, send_ref, norm_ref):
    ones = jnp.ones((8, TOK), BF16)
    norm_ref[...] = jnp.zeros_like(norm_ref)
    for h in range(H):
        feat = pk_ref[h].astype(BF16)
        put_head(send_ref, 0, h, nn(feat, v_ref[:, of_head(h // GROUP)]))
        norm_ref[h : h + 1, :] = nt(ones, feat)[0:1]
    send_ref[:, ROWS:, :] = jnp.broadcast_to(norm_ref[...][None], (NZ, PAD, DH))


def query_kernel(q_ref, v_ref, qm_ref, pk_ref, pq_ref, low_ref, rows_ref, num_ref):
    mask = causal()
    rows_ref[...] = jnp.ones_like(rows_ref)
    for h in range(H):
        pq_ref[h] = two_softmaxes(nt(qm_ref[h], q_ref[:, of_head(h)]))
    for h in range(H):
        scores = jnp.where(mask, tn(pk_ref[h].astype(BF16), pq_ref[h].astype(BF16)), 0.0)
        low_ref[h] = scores.astype(BF16)
        rows_ref[h : h + 1, :] = jnp.sum(scores, axis=0, keepdims=True)
    for h in range(H):
        num_ref[:, of_head(h)] = tn(low_ref[h], v_ref[:, of_head(h // GROUP)])


def total_kernel(got_ref, out_ref):
    total = got_ref[0]
    for j in range(1, NZ):
        total = total + got_ref[j]
    out_ref[...] = total


def from_rows(x, one_ref, two_ref, three_ref, rows, earlier):
    total = jnp.zeros((rows.stop - rows.start, DH), F32)
    for step, ref in ((1, one_ref), (2, two_ref), (3, three_ref)):
        wanted = x >= step if earlier else x < step
        total = total + jnp.where(wanted, ref[rows, :], 0.0)
    return total


STATE = slice(0, ROWS)
NORM = slice(ROWS, ROWS + PAD)


def weigh_kernel(
    x_ref, z_ref, got_ref, one_ref, two_ref, three_ref, pq_ref, rows_ref, g_ref,
    send_ref, gn_ref, rden_ref, norm_ref,
):
    x, z = x_ref[0], z_ref[0]
    state = from_rows(x, one_ref, two_ref, three_ref, STATE, True)
    norm = from_rows(x, one_ref, two_ref, three_ref, NORM, True)
    for j in range(NZ):
        send_ref[SLOT[j], STATE, :] = state
        if j < NZ - 1:
            state = state + got_ref[SLOT[j], STATE, :]
            norm = norm + jnp.where(j < z, got_ref[SLOT[j], NORM, :], 0.0)
    norm_ref[...] = norm
    columns = norm.T
    rden_ref[...] = rows_ref[...]
    for h in range(H):
        feat = pq_ref[h].astype(BF16).astype(F32)
        rden_ref[h : h + 1, :] += jnp.sum(feat * columns[:, h : h + 1], axis=0, keepdims=True)
    rden_ref[...] = 1.0 / rden_ref[...]
    scale = rden_ref[...].T
    for h in range(H):
        grad = (g_ref[:, of_head(h)].astype(F32) * scale[:, h : h + 1]).astype(BF16)
        gn_ref[:, of_head(h)] = grad
    for h in range(H):
        put_head(send_ref, ROWS, h, nn(pq_ref[h].astype(BF16), gn_ref[:, of_head(h)]))


def finish_kernel(
    got_ref, pq_ref, num_ref, rden_ref, g_ref, att_ref, sum_ref, gd_ref, low_ref, col_ref,
    out_ref,
):
    total = got_ref[0, ROWS:, :]
    for j in range(1, NZ):
        total = total + got_ref[j, ROWS:, :]
    sum_ref[STATE, :] = total
    scale = rden_ref[...].T
    col_ref[...] = jnp.zeros_like(col_ref)
    for h in range(H):
        low_ref[h] = get_head(got_ref, 0, h).astype(BF16)
    for h in range(H):
        out = num_ref[:, of_head(h)] + tn(pq_ref[h].astype(BF16), low_ref[h])
        out_ref[:, of_head(h)] = out * scale[:, h : h + 1]
    for h in range(H):
        out = out_ref[:, of_head(h)]
        att_ref[:, of_head(h)] = out.astype(BF16)
        col_ref[:, h : h + 1] = jnp.sum(g_ref[:, of_head(h)].astype(F32) * out, axis=1, keepdims=True)
    grad = -col_ref[...].T[:PAD] * rden_ref[...]
    gd_ref[...] = grad
    top = grad.astype(BF16)
    rest = grad - top.astype(F32)
    middle = rest.astype(BF16)
    bottom = (rest - middle.astype(F32)).astype(BF16)
    split = jnp.concatenate([top, middle, bottom], axis=0)
    sum_ref[NORM, :] = jnp.zeros((PAD, DH), F32)
    for h in range(H):
        parts = nt(split, pq_ref[h].astype(BF16))
        norm = parts[h : h + 1] + parts[PAD + h : PAD + h + 1] + parts[2 * PAD + h : 2 * PAD + h + 1]
        sum_ref[ROWS + h : ROWS + h + 1, :] = norm


def suffix_kernel(x_ref, z_ref, got_ref, own_ref, one_ref, two_ref, three_ref, send_ref):
    x, z = x_ref[0], z_ref[0]
    state = from_rows(x, one_ref, two_ref, three_ref, STATE, False)
    norm = from_rows(x, one_ref, two_ref, three_ref, NORM, False)
    both = norm + own_ref[NORM, :]
    for j in reversed(range(NZ)):
        send_ref[SLOT[j], STATE, :] = state
        send_ref[SLOT[j], NORM, :] = jnp.where(z > j, both, norm)
        if j > 0:
            state = state + got_ref[SLOT[j], ROWS:, :]


def inner_kernel(
    q_ref, v_ref, qm_ref, pq_ref, pk_ref, low_ref, gn_ref, gd_ref, state_ref, norm_ref,
    qg_ref, both_ref, vpart_ref, score_ref, feat_ref, gu_ref,
):
    mask = causal()
    columns = norm_ref[...].T
    for h in range(H):
        dscore = nt(v_ref[:, of_head(h // GROUP)], gn_ref[:, of_head(h)]) + gd_ref[h : h + 1, :]
        score_ref[h] = jnp.where(mask, dscore, 0.0).astype(BF16)
    for h in range(H):
        grad_feat = nn(pk_ref[h].astype(BF16), score_ref[h])
        grad_feat = grad_feat + nt(state_ref[h], gn_ref[:, of_head(h)])
        feat_ref[h] = grad_feat + columns[:, h : h + 1] * gd_ref[h : h + 1, :]
    for h in range(H):
        gu_ref[h] = back_through(pq_ref[h], feat_ref[h])
    for h in range(H):
        both_ref[h, DH:, :] = nn(gu_ref[h], q_ref[:, of_head(h)])
    for h in range(H):
        qg_ref[:, of_head(h)] = tn(gu_ref[h], qm_ref[h]).astype(BF16)
    for h in range(H):
        both_ref[h, :DH, :] = nt(pq_ref[h].astype(BF16), score_ref[h])
    for kv in range(KVH):
        heads = range(kv * GROUP, (kv + 1) * GROUP)
        vpart_ref[:, of_head(kv)] = sum(nn(low_ref[h], gn_ref[:, of_head(h)]) for h in heads)


def outer_kernel(
    core_ref, got_ref, both_ref, pk_ref, k_ref, v_ref,
    keep_ref, give_ref, gu_ref, low_ref, feat_ref,
):
    first = core_ref[0] == 0
    norm = got_ref[0, NORM, :]
    for j in range(1, NZ):
        norm = norm + got_ref[j, NORM, :]
    columns = norm.T
    for h in range(H):
        low_ref[h] = get_head(got_ref, 0, h).astype(BF16)
    for h in range(H):
        grad_feat = both_ref[h, :DH, :] + nt(low_ref[h], v_ref[:, of_head(h // GROUP)])
        feat_ref[h] = grad_feat + columns[:, h : h + 1]
    for h in range(H):
        gu_ref[h] = back_through(pk_ref[h], feat_ref[h])
    for h in range(H):
        key_weight = nn(gu_ref[h], k_ref[:, of_head(h // GROUP)])
        query_weight = both_ref[h, DH:, :]
        keep_ref[h] = jnp.where(first, query_weight, key_weight)
        give_ref[h] = jnp.where(first, key_weight, query_weight)


def last_kernel(km_ref, pk_ref, gu_ref, low_ref, vpart_ref, kg_ref, vg_ref):
    for kv in range(KVH):
        value_sum = vpart_ref[:, of_head(kv)]
        key_sum = None
        for h in range(kv * GROUP, (kv + 1) * GROUP):
            value_sum = value_sum + tn(pk_ref[h].astype(BF16), low_ref[h])
            term = tn(gu_ref[h], km_ref[h])
            key_sum = term if key_sum is None else key_sum + term
        vg_ref[:, of_head(kv)] = value_sum.astype(BF16)
        kg_ref[:, of_head(kv)] = key_sum.astype(BF16)


def run(kernel, outs, scalars, *arrays, scratch=(), macs=0):
    vmem = pl.BlockSpec(memory_space=pltpu.VMEM)
    smem = pl.BlockSpec(memory_space=pltpu.SMEM)
    moved = sum(a.size * a.dtype.itemsize for a in arrays)
    return pl.pallas_call(
        kernel,
        out_shape=tuple(jax.ShapeDtypeStruct(shape, dtype) for shape, dtype in outs),
        in_specs=[smem] * len(scalars) + [vmem] * len(arrays),
        out_specs=tuple(vmem for _ in outs),
        scratch_shapes=list(scratch),
        cost_estimate=pl.CostEstimate(
            flops=2 * macs * H * DH**3, bytes_accessed=2 * moved, transcendentals=0
        ),
        compiler_params=pltpu.CompilerParams(vmem_limit_bytes=32 * 1024 * 1024),
    )(*scalars, *arrays)


def exchange(blocks, axes):
    return lax.all_to_all(blocks, axes, 0, 0, tiled=True)


def turn(rows):
    return [lax.ppermute(rows, "x", [(i, (i + step) % NX) for i in range(NX)]) for step in (1, 2, 3)]


def exchange_z(blocks):
    return lax.all_to_all(blocks, "z", 0, 0, axis_index_groups=[list(RING)], tiled=True)


def exchange_after(blocks, token):
    return exchange_z(lax.dynamic_update_slice(blocks, token, (0, ROWS + H, 0)))


def spread(rows, count):
    return jnp.broadcast_to(rows[None], (count,) + rows.shape)


def shards(queries, key_rows, value_rows, out_grad, query_map, key_map):
    q, k, v, g = queries[0], key_rows[0], value_rows[0], out_grad[0]
    qm, km = jnp.swapaxes(query_map, 1, 2), jnp.swapaxes(key_map, 1, 2)
    x, z, core = (lax.axis_index(a).astype(jnp.int32).reshape(1) for a in ("x", "z", "core"))
    square = (H, DH, DH)
    wide = (TOK, H * DH)
    narrow = (TOK, KVH * DH)
    half = (H, FH, DH)
    small = (PAD, DH)
    flat = (ROWS + PAD, DH)
    short = (NZ,) + flat

    (pk,) = run(key_kernel, [(square, F32)], (), k, km, macs=1)
    (send,) = run(state_kernel, [(short, F32)], (), pk, v, scratch=[pltpu.VMEM(small, F32)], macs=1)
    first = lax.cond(core[0] == 0, exchange_z, lambda blocks: blocks, send)
    token = lax.ppermute(first[:1, ROWS + H :, :], "core", [(0, 1)])
    first = lax.cond(core[0] == 0, lambda blocks, token: blocks, exchange_after, first, token)
    (total,) = run(total_kernel, [(flat, F32)], (), first)
    others = turn(total)
    pq, low, rows, num = run(
        query_kernel, [(square, F32), (square, BF16), (small, F32), (wide, F32)], (), q, v, qm, pk, macs=3
    )
    send, gn, rden, norm = run(
        weigh_kernel,
        [((NZ, 2 * ROWS, DH), F32), (wide, BF16), (small, F32), (small, F32)],
        (x, z), first, *others, pq, rows, g, macs=1,
    )
    second = exchange_z(send)
    attended, total, gd, state = run(
        finish_kernel,
        [(wide, BF16), (flat, F32), (small, F32), (square, BF16)],
        (), second, pq, num, rden, g, scratch=[pltpu.VMEM((TOK, DH), F32), pltpu.VMEM(wide, F32)], macs=1,
    )
    others = turn(total)
    (send,) = run(suffix_kernel, [(short, F32)], (x, z), second, total, *others)
    third = exchange_z(send)
    query_grad, both, value_part = run(
        inner_kernel,
        [(wide, BF16), ((H, DH + FH, DH), F32), (narrow, F32)],
        (), q, v, qm, pq, pk, low, gn, gd, state, norm,
        scratch=[pltpu.VMEM(square, BF16), pltpu.VMEM(square, F32), pltpu.VMEM(half, BF16)], macs=7,
    )
    keep, give, grad_u, back = run(
        outer_kernel,
        [(half, F32), (half, F32), (half, BF16), (square, BF16)],
        (core,), third, both, pk, k, v, scratch=[pltpu.VMEM(square, F32)], macs=2,
    )
    swap = [(0, 1), (1, 0)]
    mine = keep + lax.ppermute(give, "core", swap)
    mine = exchange(mine.reshape(16, -1, DH), ("y", "x")).sum(0)
    mine = exchange_z(spread(mine, 8)).sum(0)
    mine = exchange(spread(mine, 16), ("y", "x")).reshape(half)
    key_grad, value_grad = run(
        last_kernel, [(narrow, BF16), (narrow, BF16)], (), km, pk, grad_u, back, value_part, macs=2
    )
    other = lax.ppermute(mine, "core", swap)
    query_total = jnp.where(core[0] == 0, mine, other)
    key_total = jnp.where(core[0] == 0, other, mine)
    return (
        attended[None],
        query_grad[None],
        key_grad[None],
        value_grad[None],
        jnp.swapaxes(query_total, 1, 2),
        jnp.swapaxes(key_total, 1, 2),
    )


ROWS_SPLIT = P(("y", "core"), ("x", "z"), None)


def solution(mesh):
    fine_mesh = Mesh(mesh.devices.reshape(4, 2, 4, 8), ("y", "core", "x", "z"))
    placed = (ROWS_SPLIT, ROWS_SPLIT, ROWS_SPLIT, ROWS_SPLIT, P(), P())
    return jax.shard_map(
        shards,
        mesh=fine_mesh,
        in_specs=placed,
        out_specs=placed,
        check_vma=False,
    )
```

```python
import jax
import jax.numpy as jnp
from jax import lax
from jax.experimental import pallas as pl
from jax.experimental.pallas import tpu as pltpu
from jax.sharding import Mesh, PartitionSpec as P

H = 12
KVH = 4
GROUP = H // KVH
DH = 128
FH = 64
TOK = 128
NX = 4
NZ = 8
ROWS = H * DH // NZ
PAD = 16
RING = (0, 4, 2, 6, 1, 5, 3, 7)
SLOT = [RING.index(place) for place in range(NZ)]
F32 = jnp.float32
BF16 = jnp.bfloat16


def nn(left, right):
    return lax.dot_general(left, right, (((1,), (0,)), ((), ())), preferred_element_type=F32)


def nt(left, right):
    return lax.dot_general(left, right, (((1,), (1,)), ((), ())), preferred_element_type=F32)


def tn(left, right):
    return lax.dot_general(left, right, (((0,), (0,)), ((), ())), preferred_element_type=F32)


def of_head(h):
    return slice(h * DH, (h + 1) * DH)


def pieces(h):
    row, end = h * DH, (h + 1) * DH
    while row < end:
        block, first = divmod(row, ROWS)
        count = min(ROWS - first, end - row)
        yield block, first, count, row - h * DH
        row += count


def put_head(ref, base, h, rows):
    for block, first, count, start in pieces(h):
        ref[SLOT[block], base + first : base + first + count, :] = rows[start : start + count]


def get_head(ref, base, h):
    parts = [
        ref[SLOT[block], base + first : base + first + count, :]
        for block, first, count, start in pieces(h)
    ]
    return jnp.concatenate(parts, axis=0)


def two_softmaxes(scores):
    high = jnp.exp(scores - jnp.max(scores, axis=0, keepdims=True))
    low = jnp.exp(jnp.min(scores, axis=0, keepdims=True) - scores)
    high = high * (1.0 / jnp.sum(high, axis=0, keepdims=True))
    low = low * (1.0 / jnp.sum(low, axis=0, keepdims=True))
    return jnp.concatenate([high, low], axis=0)


def causal():
    shape = (TOK, TOK)
    key = lax.broadcasted_iota(jnp.int32, shape, 0)
    query = lax.broadcasted_iota(jnp.int32, shape, 1)
    return key <= query


def back_through(prob, grad):
    p1, p2 = prob[:FH], prob[FH:]
    d1, d2 = grad[:FH], grad[FH:]
    inner1 = jnp.sum(p1 * d1, axis=0, keepdims=True)
    inner2 = jnp.sum(p2 * d2, axis=0, keepdims=True)
    return (p1 * (d1 - inner1) - p2 * (d2 - inner2)).astype(BF16)


def key_kernel(k_ref, km_ref, pk_ref):
    for h in range(H):
        pk_ref[h] = two_softmaxes(nt(km_ref[h], k_ref[:, of_head(h // GROUP)]))


def state_kernel(pk_ref, v_ref, send_ref, norm_ref):
    ones = jnp.ones((8, TOK), BF16)
    norm_ref[...] = jnp.zeros_like(norm_ref)
    for h in range(H):
        feat = pk_ref[h].astype(BF16)
        put_head(send_ref, 0, h, nn(feat, v_ref[:, of_head(h // GROUP)]))
        norm_ref[h : h + 1, :] = nt(ones, feat)[0:1]
    send_ref[:, ROWS:, :] = jnp.broadcast_to(norm_ref[...][None], (NZ, PAD, DH))


def query_kernel(q_ref, v_ref, qm_ref, pk_ref, pq_ref, low_ref, rows_ref, num_ref):
    mask = causal()
    rows_ref[...] = jnp.ones_like(rows_ref)
    for h in range(H):
        pq_ref[h] = two_softmaxes(nt(qm_ref[h], q_ref[:, of_head(h)]))
    for h in range(H):
        scores = jnp.where(mask, tn(pk_ref[h].astype(BF16), pq_ref[h].astype(BF16)), 0.0)
        low_ref[h] = scores.astype(BF16)
        rows_ref[h : h + 1, :] = jnp.sum(scores, axis=0, keepdims=True)
    for h in range(H):
        num_ref[:, of_head(h)] = tn(low_ref[h], v_ref[:, of_head(h // GROUP)])


def total_kernel(got_ref, out_ref):
    total = got_ref[0]
    for j in range(1, NZ):
        total = total + got_ref[j]
    out_ref[...] = total


def from_rows(x, one_ref, two_ref, three_ref, rows, earlier):
    total = jnp.zeros((rows.stop - rows.start, DH), F32)
    for step, ref in ((1, one_ref), (2, two_ref), (3, three_ref)):
        wanted = x >= step if earlier else x < step
        total = total + jnp.where(wanted, ref[rows, :], 0.0)
    return total


STATE = slice(0, ROWS)
NORM = slice(ROWS, ROWS + PAD)
CHUNKS = [slice(start, start + 48) for start in range(0, ROWS, 48)]


def weigh_kernel(
    x_ref, z_ref, got_ref, one_ref, two_ref, three_ref, pq_ref, rows_ref, g_ref,
    send_ref, gn_ref, rden_ref, norm_ref,
):
    x, z = x_ref[0], z_ref[0]
    norm = from_rows(x, one_ref, two_ref, three_ref, NORM, True)
    for j in range(NZ - 1):
        norm = norm + jnp.where(j < z, got_ref[SLOT[j], NORM, :], 0.0)
    norm_ref[...] = norm
    for rows in CHUNKS:
        state = from_rows(x, one_ref, two_ref, three_ref, rows, True)
        for j in range(NZ):
            send_ref[SLOT[j], rows, :] = state
            if j < NZ - 1:
                state = state + got_ref[SLOT[j], rows, :]
    columns = norm.T
    sums = [
        jnp.sum(pq_ref[h].astype(BF16).astype(F32) * columns[:, h : h + 1], axis=0, keepdims=True)
        for h in range(H)
    ]
    sums = jnp.concatenate(sums + [jnp.zeros((PAD - H, TOK), F32)], axis=0)
    inverse = 1.0 / (rows_ref[...] + sums)
    rden_ref[...] = inverse
    scale = inverse.T
    for h in range(H):
        grad = (g_ref[:, of_head(h)].astype(F32) * scale[:, h : h + 1]).astype(BF16)
        gn_ref[:, of_head(h)] = grad
    for h in range(H):
        put_head(send_ref, ROWS, h, nn(pq_ref[h].astype(BF16), gn_ref[:, of_head(h)]))


def finish_kernel(
    got_ref, pq_ref, num_ref, rden_ref, g_ref, att_ref, sum_ref, gd_ref, low_ref, col_ref,
    out_ref,
):
    total = got_ref[0, ROWS:, :]
    for j in range(1, NZ):
        total = total + got_ref[j, ROWS:, :]
    sum_ref[STATE, :] = total
    scale = rden_ref[...].T
    col_ref[...] = jnp.zeros_like(col_ref)
    for h in range(H):
        low_ref[h] = get_head(got_ref, 0, h).astype(BF16)
    for h in range(H):
        out = num_ref[:, of_head(h)] + tn(pq_ref[h].astype(BF16), low_ref[h])
        out_ref[:, of_head(h)] = out * scale[:, h : h + 1]
    for h in range(H):
        out = out_ref[:, of_head(h)]
        att_ref[:, of_head(h)] = out.astype(BF16)
        col_ref[:, h : h + 1] = jnp.sum(g_ref[:, of_head(h)].astype(F32) * out, axis=1, keepdims=True)
    grad = -col_ref[...].T[:PAD] * rden_ref[...]
    gd_ref[...] = grad
    top = grad.astype(BF16)
    rest = grad - top.astype(F32)
    middle = rest.astype(BF16)
    bottom = (rest - middle.astype(F32)).astype(BF16)
    split = jnp.concatenate([top, middle, bottom], axis=0)
    sum_ref[NORM, :] = jnp.zeros((PAD, DH), F32)
    for h in range(H):
        parts = nt(split, pq_ref[h].astype(BF16))
        norm = parts[h : h + 1] + parts[PAD + h : PAD + h + 1] + parts[2 * PAD + h : 2 * PAD + h + 1]
        sum_ref[ROWS + h : ROWS + h + 1, :] = norm


def suffix_kernel(x_ref, z_ref, got_ref, own_ref, one_ref, two_ref, three_ref, send_ref):
    x, z = x_ref[0], z_ref[0]
    state = from_rows(x, one_ref, two_ref, three_ref, STATE, False)
    norm = from_rows(x, one_ref, two_ref, three_ref, NORM, False)
    both = norm + own_ref[NORM, :]
    for j in reversed(range(NZ)):
        send_ref[SLOT[j], STATE, :] = state
        send_ref[SLOT[j], NORM, :] = jnp.where(z > j, both, norm)
        if j > 0:
            state = state + got_ref[SLOT[j], ROWS:, :]


def inner_kernel(
    q_ref, v_ref, qm_ref, pq_ref, pk_ref, low_ref, gn_ref, gd_ref, state_ref, norm_ref,
    qg_ref, both_ref, vpart_ref, score_ref, feat_ref, gu_ref,
):
    mask = causal()
    columns = norm_ref[...].T
    for h in range(H):
        dscore = nt(v_ref[:, of_head(h // GROUP)], gn_ref[:, of_head(h)]) + gd_ref[h : h + 1, :]
        score_ref[h] = jnp.where(mask, dscore, 0.0).astype(BF16)
    for h in range(H):
        grad_feat = nn(pk_ref[h].astype(BF16), score_ref[h])
        grad_feat = grad_feat + nt(state_ref[h], gn_ref[:, of_head(h)])
        feat_ref[h] = grad_feat + columns[:, h : h + 1] * gd_ref[h : h + 1, :]
    for h in range(H):
        gu_ref[h] = back_through(pq_ref[h], feat_ref[h])
    for h in range(H):
        both_ref[h, DH:, :] = nn(gu_ref[h], q_ref[:, of_head(h)])
    for h in range(H):
        qg_ref[:, of_head(h)] = tn(gu_ref[h], qm_ref[h]).astype(BF16)
    for h in range(H):
        both_ref[h, :DH, :] = nt(pq_ref[h].astype(BF16), score_ref[h])
    for kv in range(KVH):
        heads = range(kv * GROUP, (kv + 1) * GROUP)
        vpart_ref[:, of_head(kv)] = sum(nn(low_ref[h], gn_ref[:, of_head(h)]) for h in heads)


def outer_kernel(
    core_ref, got_ref, both_ref, pk_ref, k_ref, v_ref,
    keep_ref, give_ref, gu_ref, low_ref, feat_ref,
):
    first = core_ref[0] == 0
    norm = got_ref[0, NORM, :]
    for j in range(1, NZ):
        norm = norm + got_ref[j, NORM, :]
    columns = norm.T
    for h in range(H):
        low_ref[h] = get_head(got_ref, 0, h).astype(BF16)
    for h in range(H):
        grad_feat = both_ref[h, :DH, :] + nt(low_ref[h], v_ref[:, of_head(h // GROUP)])
        feat_ref[h] = grad_feat + columns[:, h : h + 1]
    for h in range(H):
        gu_ref[h] = back_through(pk_ref[h], feat_ref[h])
    for h in range(H):
        key_weight = nn(gu_ref[h], k_ref[:, of_head(h // GROUP)])
        query_weight = both_ref[h, DH:, :]
        keep_ref[h] = jnp.where(first, query_weight, key_weight)
        give_ref[h] = jnp.where(first, key_weight, query_weight)


def last_kernel(km_ref, pk_ref, gu_ref, low_ref, vpart_ref, kg_ref, vg_ref):
    for kv in range(KVH):
        heads = range(kv * GROUP, (kv + 1) * GROUP)
        total = sum(tn(pk_ref[h].astype(BF16), low_ref[h]) for h in heads)
        vg_ref[:, of_head(kv)] = (vpart_ref[:, of_head(kv)] + total).astype(BF16)
    for kv in range(KVH):
        heads = range(kv * GROUP, (kv + 1) * GROUP)
        kg_ref[:, of_head(kv)] = sum(tn(gu_ref[h], km_ref[h]) for h in heads).astype(BF16)


def run(kernel, outs, scalars, *arrays, scratch=(), macs=0):
    vmem = pl.BlockSpec(memory_space=pltpu.VMEM)
    smem = pl.BlockSpec(memory_space=pltpu.SMEM)
    moved = sum(a.size * a.dtype.itemsize for a in arrays)
    return pl.pallas_call(
        kernel,
        out_shape=tuple(jax.ShapeDtypeStruct(shape, dtype) for shape, dtype in outs),
        in_specs=[smem] * len(scalars) + [vmem] * len(arrays),
        out_specs=tuple(vmem for _ in outs),
        scratch_shapes=list(scratch),
        cost_estimate=pl.CostEstimate(
            flops=2 * macs * H * DH**3, bytes_accessed=2 * moved, transcendentals=0
        ),
        compiler_params=pltpu.CompilerParams(vmem_limit_bytes=32 * 1024 * 1024),
    )(*scalars, *arrays)


def exchange(blocks, axes):
    return lax.all_to_all(blocks, axes, 0, 0, tiled=True)


def turn(rows):
    return [lax.ppermute(rows, "x", [(i, (i + step) % NX) for i in range(NX)]) for step in (1, 2, 3)]


def exchange_z(blocks):
    return lax.all_to_all(blocks, "z", 0, 0, axis_index_groups=[list(RING)], tiled=True)


def exchange_after(blocks, token):
    return exchange_z(lax.dynamic_update_slice(blocks, token, (0, ROWS + H, 0)))


def spread(rows, count):
    return jnp.broadcast_to(rows[None], (count,) + rows.shape)


def shards(queries, key_rows, value_rows, out_grad, query_map, key_map):
    q, k, v, g = queries[0], key_rows[0], value_rows[0], out_grad[0]
    qm, km = jnp.swapaxes(query_map, 1, 2), jnp.swapaxes(key_map, 1, 2)
    x, z, core = (lax.axis_index(a).astype(jnp.int32).reshape(1) for a in ("x", "z", "core"))
    square = (H, DH, DH)
    wide = (TOK, H * DH)
    narrow = (TOK, KVH * DH)
    half = (H, FH, DH)
    small = (PAD, DH)
    flat = (ROWS + PAD, DH)
    short = (NZ,) + flat

    (pk,) = run(key_kernel, [(square, F32)], (), k, km, macs=1)
    (send,) = run(state_kernel, [(short, F32)], (), pk, v, scratch=[pltpu.VMEM(small, F32)], macs=1)
    first = lax.cond(core[0] == 0, exchange_z, lambda blocks: blocks, send)
    token = lax.ppermute(first[:1, ROWS + H :, :], "core", [(0, 1)])
    first = lax.cond(core[0] == 0, lambda blocks, token: blocks, exchange_after, first, token)
    (total,) = run(total_kernel, [(flat, F32)], (), first)
    others = turn(total)
    pq, low, rows, num = run(
        query_kernel, [(square, F32), (square, BF16), (small, F32), (wide, F32)], (), q, v, qm, pk, macs=3
    )
    send, gn, rden, norm = run(
        weigh_kernel,
        [((NZ, 2 * ROWS, DH), F32), (wide, BF16), (small, F32), (small, F32)],
        (x, z), first, *others, pq, rows, g, macs=1,
    )
    second = exchange_z(send)
    attended, total, gd, state = run(
        finish_kernel,
        [(wide, BF16), (flat, F32), (small, F32), (square, BF16)],
        (), second, pq, num, rden, g, scratch=[pltpu.VMEM((TOK, DH), F32), pltpu.VMEM(wide, F32)], macs=1,
    )
    others = turn(total)
    (send,) = run(suffix_kernel, [(short, F32)], (x, z), second, total, *others)
    third = exchange_z(send)
    query_grad, both, value_part = run(
        inner_kernel,
        [(wide, BF16), ((H, DH + FH, DH), F32), (narrow, F32)],
        (), q, v, qm, pq, pk, low, gn, gd, state, norm,
        scratch=[pltpu.VMEM(square, BF16), pltpu.VMEM(square, F32), pltpu.VMEM(half, BF16)], macs=7,
    )
    keep, give, grad_u, back = run(
        outer_kernel,
        [(half, F32), (half, F32), (half, BF16), (square, BF16)],
        (core,), third, both, pk, k, v, scratch=[pltpu.VMEM(square, F32)], macs=2,
    )
    swap = [(0, 1), (1, 0)]
    mine = keep + lax.ppermute(give, "core", swap)
    mine = exchange(mine.reshape(16, -1, DH), ("y", "x")).sum(0)
    mine = exchange_z(spread(mine, 8)).sum(0)
    mine = exchange(spread(mine, 16), ("y", "x")).reshape(half)
    key_grad, value_grad = run(
        last_kernel, [(narrow, BF16), (narrow, BF16)], (), km, pk, grad_u, back, value_part, macs=2
    )
    other = lax.ppermute(mine, "core", swap)
    query_total = jnp.where(core[0] == 0, mine, other)
    key_total = jnp.where(core[0] == 0, other, mine)
    return (
        attended[None],
        query_grad[None],
        key_grad[None],
        value_grad[None],
        jnp.swapaxes(query_total, 1, 2),
        jnp.swapaxes(key_total, 1, 2),
    )


ROWS_SPLIT = P(("y", "core"), ("x", "z"), None)


def solution(mesh):
    fine_mesh = Mesh(mesh.devices.reshape(4, 2, 4, 8), ("y", "core", "x", "z"))
    placed = (ROWS_SPLIT, ROWS_SPLIT, ROWS_SPLIT, ROWS_SPLIT, P(), P())
    return jax.shard_map(
        shards,
        mesh=fine_mesh,
        in_specs=placed,
        out_specs=placed,
        check_vma=False,
    )
```

```python
import jax
import jax.numpy as jnp
from jax import lax
from jax.experimental import pallas as pl
from jax.experimental.pallas import tpu as pltpu
from jax.sharding import Mesh, PartitionSpec as P

H = 12
KVH = 4
GROUP = H // KVH
DH = 128
FH = 64
TOK = 128
NX = 4
NZ = 8
ROWS = H * DH // NZ
PAD = 16
RING = (0, 4, 2, 6, 1, 5, 3, 7)
SLOT = [RING.index(place) for place in range(NZ)]
F32 = jnp.float32
BF16 = jnp.bfloat16


def nn(left, right):
    return lax.dot_general(left, right, (((1,), (0,)), ((), ())), preferred_element_type=F32)


def nt(left, right):
    return lax.dot_general(left, right, (((1,), (1,)), ((), ())), preferred_element_type=F32)


def tn(left, right):
    return lax.dot_general(left, right, (((0,), (0,)), ((), ())), preferred_element_type=F32)


def of_head(h):
    return slice(h * DH, (h + 1) * DH)


def pieces(h):
    row, end = h * DH, (h + 1) * DH
    while row < end:
        block, first = divmod(row, ROWS)
        count = min(ROWS - first, end - row)
        yield block, first, count, row - h * DH
        row += count


def put_head(ref, base, h, rows):
    for block, first, count, start in pieces(h):
        ref[SLOT[block], base + first : base + first + count, :] = rows[start : start + count]


def get_head(ref, base, h):
    parts = [
        ref[SLOT[block], base + first : base + first + count, :]
        for block, first, count, start in pieces(h)
    ]
    return jnp.concatenate(parts, axis=0)


def two_softmaxes(scores):
    high = jnp.exp(scores - jnp.max(scores, axis=0, keepdims=True))
    low = jnp.exp(jnp.min(scores, axis=0, keepdims=True) - scores)
    high = high * (1.0 / jnp.sum(high, axis=0, keepdims=True))
    low = low * (1.0 / jnp.sum(low, axis=0, keepdims=True))
    return jnp.concatenate([high, low], axis=0)


def causal():
    shape = (TOK, TOK)
    key = lax.broadcasted_iota(jnp.int32, shape, 0)
    query = lax.broadcasted_iota(jnp.int32, shape, 1)
    return key <= query


def back_through(prob, grad):
    p1, p2 = prob[:FH], prob[FH:]
    d1, d2 = grad[:FH], grad[FH:]
    inner1 = jnp.sum(p1 * d1, axis=0, keepdims=True)
    inner2 = jnp.sum(p2 * d2, axis=0, keepdims=True)
    return (p1 * (d1 - inner1) - p2 * (d2 - inner2)).astype(BF16)


def key_kernel(k_ref, km_ref, pk_ref):
    for h in range(H):
        pk_ref[h] = two_softmaxes(nt(km_ref[h], k_ref[:, of_head(h // GROUP)]))


def state_kernel(pk_ref, v_ref, send_ref, norm_ref):
    ones = jnp.ones((8, TOK), BF16)
    norm_ref[...] = jnp.zeros_like(norm_ref)
    for h in range(H):
        feat = pk_ref[h].astype(BF16)
        put_head(send_ref, 0, h, nn(feat, v_ref[:, of_head(h // GROUP)]))
        norm_ref[h : h + 1, :] = nt(ones, feat)[0:1]
    send_ref[:, ROWS:, :] = jnp.broadcast_to(norm_ref[...][None], (NZ, PAD, DH))


def query_kernel(q_ref, v_ref, qm_ref, pk_ref, pq_ref, low_ref, rows_ref, num_ref):
    mask = causal()
    rows_ref[...] = jnp.ones_like(rows_ref)
    for h in range(H):
        pq_ref[h] = two_softmaxes(nt(qm_ref[h], q_ref[:, of_head(h)]))
    for h in range(H):
        scores = jnp.where(mask, tn(pk_ref[h].astype(BF16), pq_ref[h].astype(BF16)), 0.0)
        low_ref[h] = scores.astype(BF16)
        rows_ref[h : h + 1, :] = jnp.sum(scores, axis=0, keepdims=True)
    for h in range(H):
        num_ref[:, of_head(h)] = tn(low_ref[h], v_ref[:, of_head(h // GROUP)])


def total_kernel(got_ref, out_ref):
    total = got_ref[0]
    for j in range(1, NZ):
        total = total + got_ref[j]
    out_ref[...] = total


def from_rows(x, one_ref, two_ref, three_ref, rows, earlier):
    total = jnp.zeros((rows.stop - rows.start, DH), F32)
    for step, ref in ((1, one_ref), (2, two_ref), (3, three_ref)):
        wanted = x >= step if earlier else x < step
        total = total + jnp.where(wanted, ref[rows, :], 0.0)
    return total


STATE = slice(0, ROWS)
NORM = slice(ROWS, ROWS + PAD)
CHUNKS = [slice(start, start + 48) for start in range(0, ROWS, 48)]


def weigh_kernel(
    x_ref, z_ref, got_ref, one_ref, two_ref, three_ref, pq_ref, rows_ref, g_ref,
    send_ref, gn_ref, rden_ref, norm_ref,
):
    x, z = x_ref[0], z_ref[0]
    norm = from_rows(x, one_ref, two_ref, three_ref, NORM, True)
    for j in range(NZ - 1):
        norm = norm + jnp.where(j < z, got_ref[SLOT[j], NORM, :], 0.0)
    norm_ref[...] = norm
    for rows in CHUNKS:
        state = from_rows(x, one_ref, two_ref, three_ref, rows, True)
        for j in range(NZ):
            send_ref[SLOT[j], rows, :] = state
            if j < NZ - 1:
                state = state + got_ref[SLOT[j], rows, :]
    columns = norm.T
    sums = [
        jnp.sum(pq_ref[h].astype(BF16).astype(F32) * columns[:, h : h + 1], axis=0, keepdims=True)
        for h in range(H)
    ]
    sums = jnp.concatenate(sums + [jnp.zeros((PAD - H, TOK), F32)], axis=0)
    inverse = 1.0 / (rows_ref[...] + sums)
    rden_ref[...] = inverse
    scale = inverse.T
    for h in range(H):
        grad = (g_ref[:, of_head(h)].astype(F32) * scale[:, h : h + 1]).astype(BF16)
        gn_ref[:, of_head(h)] = grad
    for h in range(H):
        put_head(send_ref, ROWS, h, nn(pq_ref[h].astype(BF16), gn_ref[:, of_head(h)]))


def finish_kernel(
    got_ref, pq_ref, num_ref, rden_ref, g_ref, att_ref, sum_ref, gd_ref, low_ref, col_ref,
    out_ref,
):
    total = got_ref[0, ROWS:, :]
    for j in range(1, NZ):
        total = total + got_ref[j, ROWS:, :]
    sum_ref[STATE, :] = total
    scale = rden_ref[...].T
    col_ref[...] = jnp.zeros_like(col_ref)
    for h in range(H):
        low_ref[h] = get_head(got_ref, 0, h).astype(BF16)
    for h in range(H):
        out = num_ref[:, of_head(h)] + tn(pq_ref[h].astype(BF16), low_ref[h])
        out_ref[:, of_head(h)] = out * scale[:, h : h + 1]
    for h in range(H):
        out = out_ref[:, of_head(h)]
        att_ref[:, of_head(h)] = out.astype(BF16)
        col_ref[:, h : h + 1] = jnp.sum(g_ref[:, of_head(h)].astype(F32) * out, axis=1, keepdims=True)
    grad = -col_ref[...].T[:PAD] * rden_ref[...]
    gd_ref[...] = grad
    top = grad.astype(BF16)
    rest = grad - top.astype(F32)
    middle = rest.astype(BF16)
    bottom = (rest - middle.astype(F32)).astype(BF16)
    split = jnp.concatenate([top, middle, bottom], axis=0)
    sum_ref[NORM, :] = jnp.zeros((PAD, DH), F32)
    for h in range(H):
        parts = nt(split, pq_ref[h].astype(BF16))
        norm = parts[h : h + 1] + parts[PAD + h : PAD + h + 1] + parts[2 * PAD + h : 2 * PAD + h + 1]
        sum_ref[ROWS + h : ROWS + h + 1, :] = norm


def suffix_kernel(x_ref, z_ref, got_ref, own_ref, one_ref, two_ref, three_ref, send_ref):
    x, z = x_ref[0], z_ref[0]
    state = from_rows(x, one_ref, two_ref, three_ref, STATE, False)
    norm = from_rows(x, one_ref, two_ref, three_ref, NORM, False)
    both = norm + own_ref[NORM, :]
    for j in reversed(range(NZ)):
        send_ref[SLOT[j], STATE, :] = state
        send_ref[SLOT[j], NORM, :] = jnp.where(z > j, both, norm)
        if j > 0:
            state = state + got_ref[SLOT[j], ROWS:, :]


def inner_kernel(
    q_ref, v_ref, qm_ref, pq_ref, pk_ref, low_ref, gn_ref, gd_ref, state_ref, norm_ref,
    qg_ref, both_ref, vpart_ref, score_ref, feat_ref, gu_ref,
):
    mask = causal()
    columns = norm_ref[...].T
    for h in range(H):
        dscore = nt(v_ref[:, of_head(h // GROUP)], gn_ref[:, of_head(h)]) + gd_ref[h : h + 1, :]
        score_ref[h] = jnp.where(mask, dscore, 0.0).astype(BF16)
    for h in range(H):
        grad_feat = nn(pk_ref[h].astype(BF16), score_ref[h])
        grad_feat = grad_feat + nt(state_ref[h], gn_ref[:, of_head(h)])
        feat_ref[h] = grad_feat + columns[:, h : h + 1] * gd_ref[h : h + 1, :]
    for h in range(H):
        gu_ref[h] = back_through(pq_ref[h], feat_ref[h])
    for h in range(H):
        both_ref[h, DH:, :] = nn(gu_ref[h], q_ref[:, of_head(h)])
    for h in range(H):
        qg_ref[:, of_head(h)] = tn(gu_ref[h], qm_ref[h]).astype(BF16)
    for h in range(H):
        both_ref[h, :DH, :] = nt(pq_ref[h].astype(BF16), score_ref[h])
    for kv in range(KVH):
        heads = range(kv * GROUP, (kv + 1) * GROUP)
        vpart_ref[:, of_head(kv)] = sum(nn(low_ref[h], gn_ref[:, of_head(h)]) for h in heads)


def outer_kernel(
    core_ref, got_ref, both_ref, pk_ref, k_ref, v_ref,
    keep_ref, give_ref, gu_ref, low_ref, feat_ref,
):
    first = core_ref[0] == 0
    norm = got_ref[0, NORM, :]
    for j in range(1, NZ):
        norm = norm + got_ref[j, NORM, :]
    columns = norm.T
    for h in range(H):
        low_ref[h] = get_head(got_ref, 0, h).astype(BF16)
    for h in range(H):
        grad_feat = both_ref[h, :DH, :] + nt(low_ref[h], v_ref[:, of_head(h // GROUP)])
        feat_ref[h] = grad_feat + columns[:, h : h + 1]
    for h in range(H):
        gu_ref[h] = back_through(pk_ref[h], feat_ref[h])
    for h in range(H):
        key_weight = nn(gu_ref[h], k_ref[:, of_head(h // GROUP)])
        query_weight = both_ref[h, DH:, :]
        keep_ref[h] = jnp.where(first, query_weight, key_weight)
        give_ref[h] = jnp.where(first, key_weight, query_weight)


def last_kernel(km_ref, pk_ref, gu_ref, low_ref, vpart_ref, kg_ref, vg_ref):
    for kv in range(KVH):
        heads = range(kv * GROUP, (kv + 1) * GROUP)
        total = sum(tn(pk_ref[h].astype(BF16), low_ref[h]) for h in heads)
        vg_ref[:, of_head(kv)] = (vpart_ref[:, of_head(kv)] + total).astype(BF16)
    for kv in range(KVH):
        heads = range(kv * GROUP, (kv + 1) * GROUP)
        kg_ref[:, of_head(kv)] = sum(tn(gu_ref[h], km_ref[h]) for h in heads).astype(BF16)


def run(kernel, outs, scalars, *arrays, scratch=(), macs=0):
    vmem = pl.BlockSpec(memory_space=pltpu.VMEM)
    smem = pl.BlockSpec(memory_space=pltpu.SMEM)
    moved = sum(a.size * a.dtype.itemsize for a in arrays)
    return pl.pallas_call(
        kernel,
        out_shape=tuple(jax.ShapeDtypeStruct(shape, dtype) for shape, dtype in outs),
        in_specs=[smem] * len(scalars) + [vmem] * len(arrays),
        out_specs=tuple(vmem for _ in outs),
        scratch_shapes=list(scratch),
        cost_estimate=pl.CostEstimate(
            flops=2 * macs * H * DH**3, bytes_accessed=2 * moved, transcendentals=0
        ),
        compiler_params=pltpu.CompilerParams(vmem_limit_bytes=32 * 1024 * 1024),
    )(*scalars, *arrays)


def exchange(blocks, axes):
    return lax.all_to_all(blocks, axes, 0, 0, tiled=True)


def turn(rows):
    return [lax.ppermute(rows, "x", [(i, (i + step) % NX) for i in range(NX)]) for step in (1, 2, 3)]


def exchange_z(blocks):
    return lax.all_to_all(blocks, "z", 0, 0, axis_index_groups=[list(RING)], tiled=True)


PLANE = (0, 8, 4, 12, 2, 10, 6, 14, 1, 9, 5, 13, 3, 11, 7, 15)


def exchange_yx(blocks):
    return lax.all_to_all(blocks, ("y", "x"), 0, 0, axis_index_groups=[list(PLANE)], tiled=True)


def exchange_after(blocks, token):
    return exchange_z(lax.dynamic_update_slice(blocks, token, (0, ROWS + H, 0)))


def spread(rows, count):
    return jnp.broadcast_to(rows[None], (count,) + rows.shape)


def shards(queries, key_rows, value_rows, out_grad, query_map, key_map):
    q, k, v, g = queries[0], key_rows[0], value_rows[0], out_grad[0]
    qm, km = jnp.swapaxes(query_map, 1, 2), jnp.swapaxes(key_map, 1, 2)
    x, z, core = (lax.axis_index(a).astype(jnp.int32).reshape(1) for a in ("x", "z", "core"))
    square = (H, DH, DH)
    wide = (TOK, H * DH)
    narrow = (TOK, KVH * DH)
    half = (H, FH, DH)
    small = (PAD, DH)
    flat = (ROWS + PAD, DH)
    short = (NZ,) + flat

    (pk,) = run(key_kernel, [(square, F32)], (), k, km, macs=1)
    (send,) = run(state_kernel, [(short, F32)], (), pk, v, scratch=[pltpu.VMEM(small, F32)], macs=1)
    first = lax.cond(core[0] == 0, exchange_z, lambda blocks: blocks, send)
    token = lax.ppermute(first[:1, ROWS + H :, :], "core", [(0, 1)])
    first = lax.cond(core[0] == 0, lambda blocks, token: blocks, exchange_after, first, token)
    (total,) = run(total_kernel, [(flat, F32)], (), first)
    others = turn(total)
    pq, low, rows, num = run(
        query_kernel, [(square, F32), (square, BF16), (small, F32), (wide, F32)], (), q, v, qm, pk, macs=3
    )
    send, gn, rden, norm = run(
        weigh_kernel,
        [((NZ, 2 * ROWS, DH), F32), (wide, BF16), (small, F32), (small, F32)],
        (x, z), first, *others, pq, rows, g, macs=1,
    )
    second = exchange_z(send)
    attended, total, gd, state = run(
        finish_kernel,
        [(wide, BF16), (flat, F32), (small, F32), (square, BF16)],
        (), second, pq, num, rden, g, scratch=[pltpu.VMEM((TOK, DH), F32), pltpu.VMEM(wide, F32)], macs=1,
    )
    others = turn(total)
    (send,) = run(suffix_kernel, [(short, F32)], (x, z), second, total, *others)
    third = exchange_z(send)
    query_grad, both, value_part = run(
        inner_kernel,
        [(wide, BF16), ((H, DH + FH, DH), F32), (narrow, F32)],
        (), q, v, qm, pq, pk, low, gn, gd, state, norm,
        scratch=[pltpu.VMEM(square, BF16), pltpu.VMEM(square, F32), pltpu.VMEM(half, BF16)], macs=7,
    )
    keep, give, grad_u, back = run(
        outer_kernel,
        [(half, F32), (half, F32), (half, BF16), (square, BF16)],
        (core,), third, both, pk, k, v, scratch=[pltpu.VMEM(square, F32)], macs=2,
    )
    swap = [(0, 1), (1, 0)]
    mine = keep + lax.ppermute(give, "core", swap)
    mine = exchange_yx(mine.reshape(16, -1, DH)).sum(0)
    mine = exchange_z(spread(mine, 8)).sum(0)
    mine = exchange_yx(spread(mine, 16)).reshape(half)
    key_grad, value_grad = run(
        last_kernel, [(narrow, BF16), (narrow, BF16)], (), km, pk, grad_u, back, value_part, macs=2
    )
    other = lax.ppermute(mine, "core", swap)
    query_total = jnp.where(core[0] == 0, mine, other)
    key_total = jnp.where(core[0] == 0, other, mine)
    return (
        attended[None],
        query_grad[None],
        key_grad[None],
        value_grad[None],
        jnp.swapaxes(query_total, 1, 2),
        jnp.swapaxes(key_total, 1, 2),
    )


ROWS_SPLIT = P(("y", "core"), ("x", "z"), None)


def solution(mesh):
    fine_mesh = Mesh(mesh.devices.reshape(4, 2, 4, 8), ("y", "core", "x", "z"))
    placed = (ROWS_SPLIT, ROWS_SPLIT, ROWS_SPLIT, ROWS_SPLIT, P(), P())
    return jax.shard_map(
        shards,
        mesh=fine_mesh,
        in_specs=placed,
        out_specs=placed,
        check_vma=False,
    )
```
